512 devices in a mesh: depth: 32 (over z_lo, y), height: 2 (over z_hi), view: 8 (over x, core).
Axes of the slice: x: 4, y: 8, z: 8 (z_hi: 2, z_lo: 4; z = z_hi * 4 + z_lo), core: 2. Of those that a mesh axis runs over, the one named last changes fastest.
Arguments:
- camera_feats: bfloat16 [4096, 16, 128], P(('depth', 'height', 'view')), may hold values from -6 to 6
- footprint_slot_weights: bfloat16 [8, 128, 128], replicated, may hold values from -0.1875 to 0.1875
- tile_bricks: int32 [4096, 8], P(('depth', 'height', 'view')), may hold values from 0 to 7
- tile_rows: int32 [4096, 8], P(('depth', 'height', 'view')), may hold values from 0 to 7
- conv_first: bfloat16 [16, 16, 3, 3, 3], replicated, may hold values from -0.3125 to 0.3125
- conv_second: bfloat16 [16, 16, 3, 3, 3], replicated, may hold values from -0.3125 to 0.3125
- conv_third: bfloat16 [16, 16, 3, 3, 3], replicated, may hold values from -0.3125 to 0.3125
- bias_first: float32 [16], replicated, may hold values from -3 to 3
- bias_second: float32 [16], replicated, may hold values from -3 to 3
- out_grad: bfloat16 [256, 16, 16, 128], P(('depth', 'view'), 'height'), may hold values from -6 to 6
Outputs:
- field: bfloat16 [256, 16, 16, 128], P(('depth', 'view'), 'height')
- camera_tile_feature_gradient: float32 [4096, 16, 128], P(('depth', 'height', 'view'))
- weight_grads: float32 [3, 16, 16, 3, 3, 3], replicated
- bias_gradient_pair: float32 [2, 16], replicated
The draws below stay inside these ranges and needn't reach their ends.
All inputs are finite; a program needn't handle non-finite values.
Results may differ from the reference program's by a relative error of at most 0.017.
Values may be sent and summed in bfloat16 or wider, within the bound.
No kernel may reach another device: no remote copies, remote signals or barrier semaphores. Data moves between devices by JAX's collectives and lax.ppermute only.
A program may use at most 64 MiB of HBM per device.

```python
import math
import jax
import jax.numpy as jnp
from jax import lax

C = 16
P_SIZE = 128
XB = 128
K = 8
ZP = 1
CX = 128
CY = 8
TILES = 8
NZ = 256
NY = 16
NX = 128
CAMTILES = 4096
N_DEPTH = 32
N_HEIGHT = 2
N_VIEW = 8


def draw_out_grad(key, part):
    random_key_first = jax.random.fold_in(jax.random.fold_in(key, 11), 0)
    depth_pos = jnp.arange(NZ, dtype=jnp.float32) / max(NZ - 1, 1)
    scaling = (0.5 + depth_pos)[:, None, None, None]
    noise_part = jnp.clip(jax.random.normal(random_key_first, (NZ, NY, C, NX), jnp.float32), -4.0, 4.0)
    drawn = noise_part * scaling
    return drawn.astype(jnp.bfloat16)


def with_ends(values, stream_key, least, largest):
    shape = values.shape
    place = [jax.random.randint(jax.random.fold_in(stream_key, axis), (), 0, shape[axis]) for axis in range(len(shape))]
    values = values.at[tuple(place)].set(least)
    longest = shape.index(max(shape))
    place[longest] = (place[longest] + 1) % shape[longest]
    return values.at[tuple(place)].set(largest)


def steps_of(key, extent, pieces, least, largest):
    gain, own = 1.0, jax.random.fold_in(key, 6)
    for position, shards_of in pieces:
        draws = jnp.exp(jax.random.uniform(jax.random.fold_in(own, position), (shards_of,), jnp.float32, least / len(pieces), largest / len(pieces)))
        gain = gain * jnp.repeat(draws, extent[position] // shards_of).reshape([-1 if axis == position else 1 for axis in range(len(extent))])
    return gain


def centred(key, extent, deviation, most, shards=(), held_as=jnp.bfloat16):
    entries = deviation * jax.random.normal(key, extent, jnp.float32)
    if shards:
        entries = entries * steps_of(key, extent, shards, -0.22, 0.18)
    return jnp.clip(entries, -most, most).astype(held_as)


def setup_inputs(seed: int = 0) -> dict:
    streams_of = jax.random.split(jax.random.key(seed), 11)
    return {
        "camera_feats": centred(streams_of[0], (CAMTILES, C, P_SIZE), 1.0, 6.0, ((0, 512),)),
        "footprint_slot_weights": centred(streams_of[1], (K, XB, P_SIZE), (TILES * K * P_SIZE // (ZP * CY * CX // XB)) ** -0.5, 0.1875),
        "tile_bricks": with_ends(jax.random.randint(streams_of[2], (CAMTILES, K), 0, N_VIEW), jax.random.fold_in(streams_of[2], 1), 0, N_VIEW - 1).astype(jnp.int32),
        "tile_rows": with_ends(jax.random.randint(streams_of[3], (CAMTILES, K), 0, ZP * CY * CX // XB), jax.random.fold_in(streams_of[3], 1), 0, (ZP * CY * CX // XB) - 1).astype(jnp.int32),
        "conv_first": centred(streams_of[4], (C, C, 3, 3, 3), (27 * C) ** -0.5, 0.3125),
        "conv_second": centred(streams_of[5], (C, C, 3, 3, 3), (27 * C) ** -0.5, 0.3125),
        "conv_third": centred(streams_of[6], (C, C, 3, 3, 3), (27 * C) ** -0.5, 0.3125),
        "bias_first": centred(streams_of[7], (C,), 0.5, 3.0, (), jnp.float32),
        "bias_second": centred(streams_of[8], (C,), 0.5, 3.0, (), jnp.float32),
        "out_grad": draw_out_grad(jax.random.fold_in(streams_of[10], 71), 0),
    }


conv_layout = ('NDHCW', 'OIDHW', 'NDHCW')
grad_layout = ('CDHNW', 'IDHOW', 'CNDHW')

def conv_same(volume, weight):
    result = lax.conv_general_dilated(volume[None], weight, (1, 1, 1), ((1, 1), (1, 1), (1, 1)), dimension_numbers=conv_layout, preferred_element_type=jnp.float32)
    return result[0]

def flip_swap(weight):
    return jnp.transpose(jnp.flip(weight, (2, 3, 4)), (1, 0, 2, 3, 4))

def weight_grad(grad_out, volume):
    padded = jnp.pad(volume, ((1, 1), (1, 1), (0, 0), (1, 1)))
    return lax.conv_general_dilated(padded[None], grad_out[None], (1, 1, 1), ((0, 0), (0, 0), (0, 0)), dimension_numbers=grad_layout, preferred_element_type=jnp.float32)

def silu_grad(values):
    sigma = jax.nn.sigmoid(values)
    return sigma * (1.0 + values * (1.0 - sigma))

def lift_region(region_feature_slab, bricks_region, rows_region, footprint_slot_weights):
    block_count = CX // XB
    plane_rows = bricks_region * (ZP * CY) + rows_region // block_count
    blocks = rows_region % block_count
    view_ids = jnp.arange(N_VIEW, dtype=jnp.int32)[:, None, None]
    partial_value = jnp.zeros((N_VIEW, N_VIEW * ZP * CY, C, block_count, XB), jnp.float32)
    contrib = jnp.einsum('vtcp,kxp->vtkcx', region_feature_slab.astype(jnp.float32), footprint_slot_weights.astype(jnp.float32))
    partial_value = partial_value.at[view_ids, plane_rows, :, blocks, :].add(contrib)
    rounded = lax.optimization_barrier(partial_value.astype(jnp.bfloat16)).astype(jnp.float32)
    region = lax.optimization_barrier(jnp.sum(rounded, axis=0)).astype(jnp.bfloat16)
    return region.reshape(N_VIEW * ZP, CY, C, CX)

def reference(camera_feats, footprint_slot_weights, tile_bricks, tile_rows, conv_first, conv_second, conv_third, bias_first, bias_second, out_grad):
    regions_count = N_DEPTH * N_HEIGHT
    feature_partition = camera_feats.reshape(regions_count, N_VIEW, TILES, C, P_SIZE)
    bricks_split = tile_bricks.reshape(regions_count, N_VIEW, TILES, K)
    rows_split = tile_rows.reshape(regions_count, N_VIEW, TILES, K)
    regions = lax.map(lambda items: lift_region(items[0], items[1], items[2], footprint_slot_weights), (feature_partition, bricks_split, rows_split))
    lifted = jnp.transpose(regions.reshape(N_DEPTH, N_HEIGHT, N_VIEW * ZP, CY, C, CX), (0, 2, 1, 3, 4, 5)).reshape(NZ, NY, C, CX)
    pre_first = conv_same(lifted, conv_first) + bias_first[None, None, :, None]
    act_first = jax.nn.silu(pre_first).astype(jnp.bfloat16)
    pre_second = conv_same(act_first, conv_second) + bias_second[None, None, :, None]
    act_second = (jax.nn.silu(pre_second) + act_first.astype(jnp.float32)).astype(jnp.bfloat16)
    field = conv_same(act_second, conv_third).astype(jnp.bfloat16)
    up_second = conv_same(out_grad, flip_swap(conv_third))
    slope_second = up_second * silu_grad(pre_second)
    back_second = slope_second.astype(jnp.bfloat16)
    up_first = up_second + conv_same(back_second, flip_swap(conv_second))
    slope_first = up_first * silu_grad(pre_first)
    back_first = slope_first.astype(jnp.bfloat16)
    lift_grad = conv_same(back_first, flip_swap(conv_first)).astype(jnp.bfloat16)
    block_count = CX // XB
    device_ids = jnp.arange(CAMTILES, dtype=jnp.int32) // TILES
    region_ids = device_ids // N_VIEW
    depth_ids = region_ids // N_HEIGHT
    height_index_list = region_ids % N_HEIGHT
    planes = (depth_ids[:, None] * N_VIEW + tile_bricks) * ZP + tile_rows // (CY * block_count)
    ycells = height_index_list[:, None] * CY + tile_rows // block_count % CY
    blocks = tile_rows % block_count
    grid = lift_grad.reshape(NZ, NY, C, block_count, XB)
    chosen_table_entries = grid[planes, ycells, :, blocks, :]
    camera_tile_feature_gradient = jnp.einsum('urvo,ron->uvn', chosen_table_entries.astype(jnp.float32), footprint_slot_weights.astype(jnp.float32))
    scale = 1.0 / math.sqrt(NZ * NY * NX)
    weight_grads = jnp.stack([weight_grad(back_first, lifted), weight_grad(back_second, act_first), weight_grad(out_grad, act_second)]) * scale
    bias_gradient_pair = jnp.stack([lax.optimization_barrier(jnp.sum(slope_first, axis=(0, 1, 3))), lax.optimization_barrier(jnp.sum(slope_second, axis=(0, 1, 3)))]) * scale
    return (field, camera_tile_feature_gradient, weight_grads, bias_gradient_pair)
```

```python
import math

import jax
import jax.numpy as jnp
from jax import lax
from jax.experimental import pallas as pl
from jax.experimental.pallas import tpu as pltpu
from jax.sharding import PartitionSpec as P

C = 16
X = 128
YB = 8
YC = 256
HALF = 128
RIM = 64
VIEWS = 8
F32, BF16 = jnp.float32, jnp.bfloat16
MIB = 1 << 20


def call(kernel, outs, scratch=(), vmem=32, flops=0, moved=0):
    return dict(
        out_shape=outs,
        scratch_shapes=list(scratch),
        compiler_params=pltpu.CompilerParams(vmem_limit_bytes=vmem * MIB),
        cost_estimate=pl.CostEstimate(flops=flops, bytes_accessed=moved, transcendentals=0),
    )


def vmem_spec():
    return pl.BlockSpec(memory_space=pltpu.VMEM)


def smem_spec():
    return pl.BlockSpec(memory_space=pltpu.SMEM)


def band_kernel(taps_ref, band_ref):
    at = lax.broadcasted_iota(jnp.int32, (X, YC), 0)
    to = lax.broadcasted_iota(jnp.int32, (X, YC), 1)
    for y in range(16):
        spread = jnp.where(to == at + (y - 1) * C, 1.0, 0.0).astype(BF16)
        rows = jnp.dot(taps_ref[...], spread, preferred_element_type=F32).astype(BF16)
        for n in range(6):
            for a in range(3):
                for c in range(3):
                    first = ((n * 3 + a) * 3 + c) * C
                    band_ref[n, a, y * C : (y + 1) * C, c * YC : (c + 1) * YC] = rows[
                        first : first + C, :
                    ]


def lift_kernel(bricks_ref, rows_ref, feats_ref, weights_ref, out_ref, total):
    total[...] = jnp.zeros_like(total)
    tiles, slots = bricks_ref.shape
    for k in range(slots):
        blocks = lax.dot_general(
            feats_ref[...], weights_ref[k], (((1,), (1,)), ((), ())), preferred_element_type=F32
        )
        for t in range(tiles):
            row = bricks_ref[t, k] * YB + rows_ref[t, k]
            total[row] += blocks[t * C : (t + 1) * C, :]
    out_ref[...] = total[...].astype(BF16).reshape(out_ref.shape)


def camera_kernel(bricks_ref, rows_ref, arrived_ref, weights_ref, out_ref, chosen):
    tiles, slots = bricks_ref.shape
    for k in range(slots):
        for t in range(tiles):
            at = pl.multiple_of(rows_ref[t, k] * C, C)
            chosen[t * C : (t + 1) * C, k * X : (k + 1) * X] = arrived_ref[
                bricks_ref[t, k], pl.ds(at, C), :
            ]
    out_ref[...] = jnp.dot(
        chosen[...], weights_ref[...].reshape(slots * X, X), preferred_element_type=F32
    )


def silu_and_slope(v):
    s = jax.nn.sigmoid(v)
    return v * s, s * (1.0 + v * (1.0 - s))


def main_kernel(
    arrived_ref,
    band_ref,
    bias_ref,
    field_ref,
    payload_ref,
    s_lift,
    s_grad,
    s_act1,
    s_act2,
    s_back2,
    s_back1,
    slope1,
    slope2,
    up2,
):
    depth, height, view = (lax.axis_index(n) for n in ("depth", "height", "view"))
    lane = lax.broadcasted_iota(jnp.int32, (YC, X), 1)
    first_lane, last_lane = lane == 0, lane == X - 1
    low = height == 0

    def put(dst, index, plane):
        cols = slice(index * X, (index + 1) * X)
        dst[0:YC, cols] = jnp.where(first_lane, 0.0, pltpu.roll(plane, 1, 1)).astype(BF16)
        dst[YC : 2 * YC, cols] = plane.astype(BF16)
        dst[2 * YC : 3 * YC, cols] = jnp.where(last_lane, 0.0, pltpu.roll(plane, X - 1, 1)).astype(
            BF16
        )

    def fetch(offset, kind):
        source = lax.rem(view + offset + VIEWS, VIEWS)
        if offset == -4:
            kind = jnp.where(view < 4, 1, 0)
        if offset == 4:
            kind = jnp.where(view < 4, 0, 1)
        part = arrived_ref[source, kind].astype(F32)
        own, rim = part[:HALF], part[HALF:]
        none = jnp.zeros((RIM, X), F32)
        return jnp.where(
            low,
            jnp.concatenate([own, rim, none], axis=0),
            jnp.concatenate([none, rim, own], axis=0),
        )

    def inside(offset):
        z = depth * VIEWS + view + offset
        return jnp.logical_and(z >= 0, z < lax.axis_size("depth") * VIEWS)

    def masked(offset, plane):
        return jnp.where(inside(offset), plane, 0.0)

    def conv(n, src, start, count):
        out = jnp.zeros((YC, count * X), F32)
        for a in range(3):
            out += jnp.dot(
                band_ref[n, a],
                src[:, (start + a) * X : (start + a + count) * X],
                preferred_element_type=F32,
            )
        return [out[:, i * X : (i + 1) * X] for i in range(count)]

    def pairs(count):
        return [(i, min(2, count - i)) for i in range(0, count, 2)]

    for i in range(9):
        put(s_lift, i, fetch(i - 4, 0))
    for i in range(7):
        put(s_grad, i, fetch(i - 3, 2))

    bias1, bias2 = bias_ref[0], bias_ref[1]
    for i, n in pairs(7):
        for j, pre in enumerate(conv(0, s_lift, i, n)):
            act, slope = silu_and_slope(pre + bias1)
            put(s_act1, i + j, masked(i + j - 3, act))
            if abs(i + j - 3) <= 1:
                slope1[i + j - 2] = slope
    for i, n in pairs(5):
        for j, up in enumerate(conv(3, s_grad, i, n)):
            up2[i + j] = up
    for i, n in pairs(5):
        for j, pre in enumerate(conv(1, s_act1, i, n)):
            at = i + j
            act, slope = silu_and_slope(pre + bias2)
            back = up2[at] * slope
            put(s_back2, at, masked(at - 2, back))
            if at == 2:
                slope2[...] = back
            if abs(at - 2) <= 1:
                before = s_act1[YC : 2 * YC, (at + 1) * X : (at + 2) * X].astype(F32)
                put(s_act2, at - 1, masked(at - 2, act + before))
    for i, n in pairs(3):
        for j, up in enumerate(conv(4, s_back2, i, n)):
            at = i + j
            back = (up2[at + 1] + up) * slope1[at]
            if at == 1:
                slope1[at] = back
            put(s_back1, at, masked(at - 1, back))

    def own_rows(plane):
        return jnp.where(low, plane[:HALF], plane[HALF:])

    (lift_grad,) = conv(5, s_back1, 0, 1)
    lift_grad = own_rows(lift_grad).astype(BF16)
    for v in range(VIEWS):
        payload_ref[v, :HALF, :] = lift_grad
    (field,) = conv(2, s_act2, 0, 1)
    field_ref[...] = own_rows(field).astype(BF16)

    own_at = pl.multiple_of(YC + height * HALF, HALF)
    wide = (HALF, 3 * YC)
    row_y = lax.broadcasted_iota(jnp.int32, wide, 0) // C + height * YB
    col_y = lax.rem(lax.broadcasted_iota(jnp.int32, wide, 1), YC) // C
    bands = [col_y == row_y + (b - 1) for b in range(3)]
    group = lax.broadcasted_iota(jnp.int32, (3 * C, X), 1) // C
    packed = [jnp.zeros((3 * C, X), F32) for _ in range(4)]
    layers = ((s_back1, 1, s_lift, 4), (s_back2, 2, s_act1, 3), (s_grad, 3, s_act2, 1))
    for layer, (g_ref, g_at, v_ref, v_at) in enumerate(layers):
        g = g_ref[pl.ds(own_at, HALF), g_at * X : (g_at + 1) * X]
        for a in range(3):
            at = v_at + a - 1
            products = lax.dot_general(
                g,
                v_ref[:, at * X : (at + 1) * X],
                (((1,), (1,)), ((), ())),
                preferred_element_type=F32,
            )
            by_row = [
                jnp.where(band, products, 0.0).reshape(YB, C, 3 * YC).sum(axis=0) for band in bands
            ]
            by_row = jnp.concatenate(by_row, axis=0)
            for c in range(3):
                part = by_row[:, c * YC : c * YC + X] + by_row[:, c * YC + X : (c + 1) * YC]
                for step in (64, 32, 16):
                    part = part + pltpu.roll(part, step, 1)
                q = (layer * 3 + a) * 3 + c
                packed[q // 8] = jnp.where(group == q % 8, part, packed[q // 8])
    for layer, plane in enumerate((slope1[1], slope2[...])):
        sums = jnp.sum(own_rows(plane), axis=1, keepdims=True)
        sums = jnp.broadcast_to(sums, (HALF, X)).reshape(YB, C, X).sum(axis=0)
        packed[3] = jnp.where(group == 3 + layer, jnp.concatenate([sums] * 3, axis=0), packed[3])
    for v in range(VIEWS):
        start = (v % 2) * 24
        rows = packed[v // 2][start : start + 24]
        high = rows.astype(BF16).astype(F32)
        both = jnp.concatenate([high, rows - high], axis=0)
        payload_ref[v, HALF:, :] = both.astype(BF16)


def main_call(arrived, bands, bias):
    return pl.pallas_call(
        main_kernel,
        in_specs=[vmem_spec()] * 3,
        out_specs=[vmem_spec()] * 2,
        **call(
            main_kernel,
            (
                jax.ShapeDtypeStruct((HALF, X), BF16),
                jax.ShapeDtypeStruct((VIEWS, HALF + 48, X), BF16),
            ),
            [pltpu.VMEM((3 * YC, n * X), BF16) for n in (9, 7, 7, 3, 5, 3)]
            + [
                pltpu.VMEM((3, YC, X), F32),
                pltpu.VMEM((YC, X), F32),
                pltpu.VMEM((5, YC, X), F32),
            ],
            vmem=40,
            flops=10**10,
            moved=10**7,
        ),
    )(arrived, bands, bias)


def flip_swap(weight):
    return jnp.transpose(jnp.flip(weight, (2, 3, 4)), (1, 0, 2, 3, 4))


def for_each(block, axes):
    peers = lax.axis_size(axes)
    tiles = jnp.broadcast_to(block[None], (peers, *block.shape))
    return lax.all_to_all(tiles, axes, 0, 0, tiled=True)


def body(
    camera_feats,
    footprint_slot_weights,
    tile_bricks,
    tile_rows,
    conv_first,
    conv_second,
    conv_third,
    bias_first,
    bias_second,
    out_grad,
):
    depths, heights, views = (lax.axis_size(n) for n in ("depth", "height", "view"))
    height, view = lax.axis_index("height"), lax.axis_index("view")
    tiles, slots = tile_bricks.shape

    partial = pl.pallas_call(
        lift_kernel,
        in_specs=[smem_spec(), smem_spec(), vmem_spec(), vmem_spec()],
        out_specs=vmem_spec(),
        **call(
            lift_kernel,
            jax.ShapeDtypeStruct((views, HALF, X), BF16),
            [pltpu.VMEM((views * YB, C, X), F32)],
            flops=10**8,
            moved=10**6,
        ),
    )(tile_bricks, tile_rows, camera_feats.reshape(tiles * C, X), footprint_slot_weights)
    pieces = lax.all_to_all(partial, "view", 0, 0, tiled=True)

    convs = [conv_first, conv_second, conv_third]
    convs = jnp.stack(convs + [flip_swap(w) for w in reversed(convs)])
    taps = jnp.transpose(convs, (0, 3, 5, 1, 4, 2)).reshape(-1, 3 * C)
    taps = jnp.pad(taps, ((0, 0), (0, X - 3 * C)))
    bands = pl.pallas_call(
        band_kernel,
        in_specs=[vmem_spec()],
        out_specs=vmem_spec(),
        **call(
            band_kernel,
            jax.ShapeDtypeStruct((6, 3, YC, 3 * YC), BF16),
            flops=10**9,
            moved=7 * 10**6,
        ),
    )(taps)
    bias = jnp.stack([jnp.tile(b, 16) for b in (bias_first, bias_second)])[:, :, None]

    lifted = pieces.astype(F32).sum(axis=0).astype(BF16)
    own = jnp.stack([lifted, out_grad.reshape(HALF, X)])
    moves = []
    for d in range(depths):
        for v in range(views):
            to = d + (1 if v >= views // 2 else -1)
            if 0 <= to < depths:
                moves.append((d * views + v, to * views + v))
    far = lax.ppermute(own, ("depth", "view"), moves)
    planes = jnp.concatenate([own, far])
    facing = jnp.where(height == 0, planes[:, HALF - RIM :], planes[:, :RIM])
    rim = lax.ppermute(facing, "height", [(0, 1), (1, 0)])
    planes = jnp.concatenate([planes, rim], axis=1)
    near = jnp.abs(lax.iota(jnp.int32, views) - view) <= views // 2
    near = near[:, None, None]
    parts = jnp.stack(
        [
            jnp.where(near, planes[0], planes[2]),
            jnp.broadcast_to(planes[2], (views, *planes[2].shape)),
            jnp.where(near, planes[1], planes[3]),
        ],
        axis=1,
    )
    arrived = lax.all_to_all(parts, "view", 0, 0, tiled=True)

    field, payload = main_call(arrived, bands, bias)
    arrived = lax.all_to_all(payload, "view", 0, 0, tiled=True)

    sums = arrived[:, HALF:].astype(F32).sum(axis=0)
    sums = sums[:24] + sums[24:]
    sums = for_each(sums, ("depth", "height")).sum(axis=0)

    camera_grad = pl.pallas_call(
        camera_kernel,
        in_specs=[smem_spec(), smem_spec(), vmem_spec(), vmem_spec()],
        out_specs=vmem_spec(),
        **call(
            camera_kernel,
            jax.ShapeDtypeStruct((tiles * C, X), F32),
            [pltpu.VMEM((tiles * C, slots * X), BF16)],
            flops=10**8,
            moved=10**6,
        ),
    )(tile_bricks, tile_rows, arrived, footprint_slot_weights)

    sums = for_each(sums, "view").reshape(4, 3, C, 8, C)
    scale = 1.0 / math.sqrt(YB * X * depths * heights * views)
    sums = sums * scale
    bias_gradient_pair = jnp.transpose(sums[3, 0, :, 3:5, 0])
    sums = jnp.transpose(sums, (0, 3, 2, 4, 1)).reshape(32, C, C, 3)[:27]
    weight_grads = jnp.transpose(sums.reshape(3, 3, 3, C, C, 3), (0, 3, 4, 1, 5, 2))
    return (
        field.reshape(1, YB, C, X),
        camera_grad.reshape(tiles, C, X),
        weight_grads,
        bias_gradient_pair,
    )


def solution(mesh):
    in_specs = (
        P(("depth", "height", "view"), None, None),
        P(),
        P(("depth", "height", "view"), None),
        P(("depth", "height", "view"), None),
        P(),
        P(),
        P(),
        P(),
        P(),
        P(("depth", "view"), "height", None, None),
    )
    out_specs = (
        P(("depth", "view"), "height", None, None),
        P(("depth", "height", "view"), None, None),
        P(),
        P(),
    )
    return jax.shard_map(body, mesh=mesh, in_specs=in_specs, out_specs=out_specs, check_vma=False)
```

```python
import functools
import math

import jax
import jax.numpy as jnp
from jax import lax
from jax.experimental import pallas as pl
from jax.experimental.pallas import tpu as pltpu
from jax.sharding import PartitionSpec as P

C = 16
X = 128
YB = 8
YC = 256
HALF = 128
RIM = 64
VIEWS = 8
F32, BF16 = jnp.float32, jnp.bfloat16
MIB = 1 << 20


def call(kernel, outs, scratch=(), vmem=32, flops=0, moved=0):
    return dict(
        out_shape=outs,
        scratch_shapes=list(scratch),
        compiler_params=pltpu.CompilerParams(vmem_limit_bytes=vmem * MIB),
        cost_estimate=pl.CostEstimate(flops=flops, bytes_accessed=moved, transcendentals=0),
    )


def vmem_spec():
    return pl.BlockSpec(memory_space=pltpu.VMEM)


def hbm_spec():
    return pl.BlockSpec(memory_space=pltpu.HBM)


def smem_spec():
    return pl.BlockSpec(memory_space=pltpu.SMEM)


def band_kernel(taps_ref, band_ref):
    at = lax.broadcasted_iota(jnp.int32, (X, YC), 0)
    to = lax.broadcasted_iota(jnp.int32, (X, YC), 1)
    for y in range(16):
        spread = jnp.where(to == at + (y - 1) * C, 1.0, 0.0).astype(BF16)
        rows = jnp.dot(taps_ref[...], spread, preferred_element_type=F32).astype(BF16)
        for n in range(6):
            for a in range(3):
                for c in range(3):
                    first = ((n * 3 + a) * 3 + c) * C
                    band_ref[n, a, y * C : (y + 1) * C, c * YC : (c + 1) * YC] = rows[
                        first : first + C, :
                    ]


def lift_kernel(targets_ref, feats_hbm, weights_hbm, out_ref, feats, weights, total, sems):
    fetch_feats = pltpu.make_async_copy(feats_hbm, feats, sems.at[0])
    fetch_weights = pltpu.make_async_copy(weights_hbm, weights, sems.at[1])
    fetch_feats.start()
    fetch_weights.start()
    total[...] = jnp.zeros_like(total)
    tiles, slots = targets_ref.shape
    fetch_feats.wait()
    fetch_weights.wait()
    for k in range(slots):
        blocks = lax.dot_general(
            feats[...], weights[k], (((1,), (1,)), ((), ())), preferred_element_type=F32
        )
        for t in range(tiles):
            total[targets_ref[t, k]] += blocks[t * C : (t + 1) * C, :]
    out_ref[...] = total[...].astype(BF16).reshape(out_ref.shape)


def camera_kernel(targets_ref, arrived_ref, weights_ref, out_ref, chosen):
    tiles, slots = targets_ref.shape
    for k in range(slots):
        for t in range(tiles):
            target = targets_ref[t, k]
            at = pl.multiple_of(lax.rem(target, YB) * C, C)
            chosen[t * C : (t + 1) * C, k * X : (k + 1) * X] = arrived_ref[
                lax.div(target, YB), pl.ds(at, C), :
            ]
    out_ref[...] = jnp.dot(
        chosen[...], weights_ref[...].reshape(slots * X, X), preferred_element_type=F32
    )


def spread_kernel(scale, sums_ref, weight_ref, bias_ref):
    for q in range(27):
        layer, a, c = q // 9, q // 3 % 3, q % 3
        for b in range(3):
            row = (q // 8 * 3 + b) * C
            block = sums_ref[row : row + C, q % 8 * C : (q % 8 + 1) * C]
            weight_ref[((layer * 3 + a) * 3 + b) * 3 + c] = block * scale
    for layer in range(2):
        lanes = slice((3 + layer) * C, (4 + layer) * C)
        bias_ref[layer : layer + 1, :] = sums_ref[9 * C : 9 * C + 1, lanes] * scale


def silu_and_slope(v):
    s = jax.nn.sigmoid(v)
    return v * s, s * (1.0 + v * (1.0 - s))


def main_kernel(
    arrived_ref,
    band_hbm,
    bias_ref,
    field_ref,
    payload_ref,
    s_lift,
    s_grad,
    s_act1,
    s_act2,
    s_back2,
    s_back1,
    slope1,
    slope2,
    up2,
    band_ref,
    sems,
):
    fetches = [pltpu.make_async_copy(band_hbm.at[n], band_ref.at[n], sems.at[n]) for n in range(6)]
    for n in (0, 3, 1, 4, 5, 2):
        fetches[n].start()
    depth, height, view = (lax.axis_index(n) for n in ("depth", "height", "view"))
    lane = lax.broadcasted_iota(jnp.int32, (YC, X), 1)
    first_lane, last_lane = lane == 0, lane == X - 1
    low = height == 0

    def put(dst, index, plane):
        cols = slice(index * X, (index + 1) * X)
        dst[0:YC, cols] = jnp.where(first_lane, 0.0, pltpu.roll(plane, 1, 1)).astype(BF16)
        dst[YC : 2 * YC, cols] = plane.astype(BF16)
        dst[2 * YC : 3 * YC, cols] = jnp.where(last_lane, 0.0, pltpu.roll(plane, X - 1, 1)).astype(
            BF16
        )

    def fetch(offset, kind):
        source = lax.rem(view + offset + VIEWS, VIEWS)
        if offset == -4:
            kind = jnp.where(view < VIEWS // 2, 1, 0)
        if offset == 4:
            kind = jnp.where(view < VIEWS // 2, 0, 1)
        part = arrived_ref[source, kind].astype(F32)
        own, rim = part[:HALF], part[HALF:]
        none = jnp.zeros((RIM, X), F32)
        return jnp.where(
            low,
            jnp.concatenate([own, rim, none], axis=0),
            jnp.concatenate([none, rim, own], axis=0),
        )

    def inside(offset):
        z = depth * VIEWS + view + offset
        return jnp.logical_and(z >= 0, z < lax.axis_size("depth") * VIEWS)

    def masked(offset, plane):
        return jnp.where(inside(offset), plane, 0.0)

    def conv(n, src, start, count):
        out = jnp.zeros((YC, count * X), F32)
        for a in range(3):
            out += jnp.dot(
                band_ref[n, a],
                src[:, (start + a) * X : (start + a + count) * X],
                preferred_element_type=F32,
            )
        return [out[:, i * X : (i + 1) * X] for i in range(count)]

    def pairs(count):
        return [(i, min(2, count - i)) for i in range(0, count, 2)]

    for i in range(9):
        put(s_lift, i, fetch(i - 4, 0))
    for i in range(7):
        put(s_grad, i, fetch(i - 3, 1))

    bias1, bias2 = bias_ref[0], bias_ref[1]
    fetches[0].wait()
    for i, n in pairs(7):
        for j, pre in enumerate(conv(0, s_lift, i, n)):
            act, slope = silu_and_slope(pre + bias1)
            put(s_act1, i + j, masked(i + j - 3, act))
            if abs(i + j - 3) <= 1:
                slope1[i + j - 2] = slope
    fetches[3].wait()
    for i, n in pairs(5):
        for j, up in enumerate(conv(3, s_grad, i, n)):
            up2[i + j] = up
    fetches[1].wait()
    for i, n in pairs(5):
        for j, pre in enumerate(conv(1, s_act1, i, n)):
            at = i + j
            act, slope = silu_and_slope(pre + bias2)
            back = up2[at] * slope
            put(s_back2, at, masked(at - 2, back))
            if at == 2:
                slope2[...] = back
            if abs(at - 2) <= 1:
                before = s_act1[YC : 2 * YC, (at + 1) * X : (at + 2) * X].astype(F32)
                put(s_act2, at - 1, masked(at - 2, act + before))
    fetches[4].wait()
    for i, n in pairs(3):
        for j, up in enumerate(conv(4, s_back2, i, n)):
            at = i + j
            back = (up2[at + 1] + up) * slope1[at]
            if at == 1:
                slope1[at] = back
            put(s_back1, at, masked(at - 1, back))

    def own_rows(plane):
        return jnp.where(low, plane[:HALF], plane[HALF:])

    fetches[5].wait()
    (lift_grad,) = conv(5, s_back1, 0, 1)
    lift_grad = own_rows(lift_grad).astype(BF16)
    for v in range(VIEWS):
        payload_ref[v, :HALF, :] = lift_grad
    fetches[2].wait()
    (field,) = conv(2, s_act2, 0, 1)
    field_ref[...] = own_rows(field).astype(BF16)

    own_at = pl.multiple_of(YC + height * HALF, HALF)
    wide = (HALF, 3 * YC)
    row_y = lax.broadcasted_iota(jnp.int32, wide, 0) // C + height * YB
    col_y = lax.rem(lax.broadcasted_iota(jnp.int32, wide, 1), YC) // C
    bands = [col_y == row_y + (b - 1) for b in range(3)]
    group = lax.broadcasted_iota(jnp.int32, (3 * C, X), 1) // C
    packed = [jnp.zeros((3 * C, X), F32) for _ in range(4)]
    layers = ((s_back1, 1, s_lift, 4), (s_back2, 2, s_act1, 3), (s_grad, 3, s_act2, 1))
    for layer, (g_ref, g_at, v_ref, v_at) in enumerate(layers):
        g = g_ref[pl.ds(own_at, HALF), g_at * X : (g_at + 1) * X]
        for a in range(3):
            at = v_at + a - 1
            products = lax.dot_general(
                g,
                v_ref[:, at * X : (at + 1) * X],
                (((1,), (1,)), ((), ())),
                preferred_element_type=F32,
            )
            by_row = [
                jnp.where(band, products, 0.0).reshape(YB, C, 3 * YC).sum(axis=0) for band in bands
            ]
            by_row = jnp.concatenate(by_row, axis=0)
            for c in range(3):
                part = by_row[:, c * YC : c * YC + X] + by_row[:, c * YC + X : (c + 1) * YC]
                for step in (64, 32, 16):
                    part = part + pltpu.roll(part, step, 1)
                q = (layer * 3 + a) * 3 + c
                packed[q // 8] = jnp.where(group == q % 8, part, packed[q // 8])
    for layer, plane in enumerate((slope1[1], slope2[...])):
        sums = jnp.sum(own_rows(plane), axis=1, keepdims=True)
        sums = jnp.broadcast_to(sums, (HALF, X)).reshape(YB, C, X).sum(axis=0)
        out_at = lax.broadcasted_iota(jnp.int32, (C, X), 0)
        to = lax.rem(lax.broadcasted_iota(jnp.int32, (C, X), 1), C)
        sums = jnp.sum(jnp.where(out_at == to, sums, 0.0), axis=0, keepdims=True)
        packed[3] = jnp.where(group == 3 + layer, jnp.broadcast_to(sums, (3 * C, X)), packed[3])
    for v in range(VIEWS):
        start = (v % 2) * 24
        rows = packed[v // 2][start : start + 24]
        high = rows.astype(BF16).astype(F32)
        both = jnp.concatenate([high, rows - high], axis=0)
        payload_ref[v, HALF:, :] = both.astype(BF16)


def main_call(arrived, bands, bias):
    return pl.pallas_call(
        main_kernel,
        in_specs=[vmem_spec(), hbm_spec(), vmem_spec()],
        out_specs=[vmem_spec()] * 2,
        **call(
            main_kernel,
            (
                jax.ShapeDtypeStruct((HALF, X), BF16),
                jax.ShapeDtypeStruct((VIEWS, HALF + 48, X), BF16),
            ),
            [pltpu.VMEM((3 * YC, n * X), BF16) for n in (9, 7, 7, 3, 5, 3)]
            + [
                pltpu.VMEM((3, YC, X), F32),
                pltpu.VMEM((YC, X), F32),
                pltpu.VMEM((5, YC, X), F32),
                pltpu.VMEM((6, 3, YC, 3 * YC), BF16),
                pltpu.SemaphoreType.DMA((6,)),
            ],
            vmem=40,
            flops=10**10,
            moved=10**7,
        ),
    )(arrived, bands, bias)


def flip_swap(weight):
    return jnp.transpose(jnp.flip(weight, (2, 3, 4)), (1, 0, 2, 3, 4))


def for_each(block, axes, groups=None):
    peers = len(groups[0]) if groups else lax.axis_size(axes)
    tiles = jnp.broadcast_to(block[None], (peers, *block.shape))
    return lax.all_to_all(tiles, axes, 0, 0, axis_index_groups=groups, tiled=True)


def body(
    camera_feats,
    footprint_slot_weights,
    tile_bricks,
    tile_rows,
    conv_first,
    conv_second,
    conv_third,
    bias_first,
    bias_second,
    out_grad,
):
    depths, heights, views = (lax.axis_size(n) for n in ("depth", "height", "view"))
    height, view = lax.axis_index("height"), lax.axis_index("view")
    tiles, slots = tile_bricks.shape

    targets = tile_bricks * YB + tile_rows
    partial = pl.pallas_call(
        lift_kernel,
        in_specs=[smem_spec(), hbm_spec(), hbm_spec()],
        out_specs=vmem_spec(),
        **call(
            lift_kernel,
            jax.ShapeDtypeStruct((views, HALF, X), BF16),
            [
                pltpu.VMEM((tiles * C, X), BF16),
                pltpu.VMEM((slots, X, X), BF16),
                pltpu.VMEM((views * YB, C, X), F32),
                pltpu.SemaphoreType.DMA((2,)),
            ],
            flops=10**8,
            moved=10**6,
        ),
    )(targets, camera_feats.reshape(tiles * C, X), footprint_slot_weights)
    pieces = lax.all_to_all(partial, "view", 0, 0, tiled=True)

    convs = [conv_first, conv_second, conv_third]
    convs = jnp.stack(convs + [flip_swap(w) for w in reversed(convs)])
    taps = jnp.transpose(convs, (0, 3, 5, 1, 4, 2)).reshape(-1, 3 * C)
    taps = jnp.pad(taps, ((0, 0), (0, X - 3 * C)))
    bands = pl.pallas_call(
        band_kernel,
        in_specs=[vmem_spec()],
        out_specs=vmem_spec(),
        **call(
            band_kernel,
            jax.ShapeDtypeStruct((6, 3, YC, 3 * YC), BF16),
            flops=10**9,
            moved=7 * 10**6,
        ),
    )(taps)
    bias = jnp.stack([jnp.tile(b, 16) for b in (bias_first, bias_second)])[:, :, None]

    lifted = pieces.astype(F32).sum(axis=0).astype(BF16)
    own = jnp.stack([lifted, out_grad.reshape(HALF, X)])
    moves = []
    for d in range(depths):
        for v in range(views):
            to = d + (1 if v >= views // 2 else -1)
            if 0 <= to < depths:
                moves.append((d * views + v, to * views + v))
    far = lax.ppermute(own, ("depth", "view"), moves)
    planes = jnp.concatenate([own, far])
    facing = jnp.where(height == 0, planes[:, HALF - RIM :], planes[:, :RIM])
    rim = lax.ppermute(facing, "height", [(0, 1), (1, 0)])
    planes = jnp.concatenate([planes, rim], axis=1)
    away = jnp.abs(lax.iota(jnp.int32, views) - view)[:, None, None]
    half = views // 2
    own_grad = jnp.where(away < half, planes[1], planes[3])
    parts = jnp.stack(
        [
            jnp.where(away <= half, planes[0], planes[2]),
            jnp.where(away == half, planes[2], own_grad),
        ],
        axis=1,
    )
    arrived = lax.all_to_all(parts, "view", 0, 0, tiled=True)

    field, payload = main_call(arrived, bands, bias)
    arrived = lax.all_to_all(payload, "view", 0, 0, tiled=True)

    sums = arrived[:, HALF:].astype(F32).sum(axis=0)
    sums = sums[:24] + sums[24:]
    run = views
    rings = [list(range(i, i + run)) for i in range(0, depths, run)]
    sums = for_each(sums, "depth", rings).sum(axis=0)
    rings = [
        [(i * run + j) * heights + h for h in range(heights) for i in range(depths // run)]
        for j in range(run)
    ]
    sums = for_each(sums, ("depth", "height"), rings).sum(axis=0)

    camera_grad = pl.pallas_call(
        camera_kernel,
        in_specs=[smem_spec(), vmem_spec(), vmem_spec()],
        out_specs=vmem_spec(),
        **call(
            camera_kernel,
            jax.ShapeDtypeStruct((tiles * C, X), F32),
            [pltpu.VMEM((tiles * C, slots * X), BF16)],
            flops=10**8,
            moved=10**6,
        ),
    )(targets, arrived, footprint_slot_weights)

    sums = for_each(sums, "view").reshape(12 * C, X)
    scale = 1.0 / math.sqrt(YB * X * depths * heights * views)
    weight_grads, bias_gradient_pair = pl.pallas_call(
        functools.partial(spread_kernel, scale),
        in_specs=[vmem_spec()],
        out_specs=[vmem_spec()] * 2,
        **call(
            spread_kernel,
            (jax.ShapeDtypeStruct((81, C, C), F32), jax.ShapeDtypeStruct((2, C), F32)),
        ),
    )(sums)
    weight_grads = jnp.transpose(weight_grads.reshape(3, 3, 3, 3, C, C), (0, 4, 5, 1, 2, 3))
    return (
        field.reshape(1, YB, C, X),
        camera_grad.reshape(tiles, C, X),
        weight_grads,
        bias_gradient_pair,
    )


def solution(mesh):
    in_specs = (
        P(("depth", "height", "view"), None, None),
        P(),
        P(("depth", "height", "view"), None),
        P(("depth", "height", "view"), None),
        P(),
        P(),
        P(),
        P(),
        P(),
        P(("depth", "view"), "height", None, None),
    )
    out_specs = (
        P(("depth", "view"), "height", None, None),
        P(("depth", "height", "view"), None, None),
        P(),
        P(),
    )
    return jax.shard_map(body, mesh=mesh, in_specs=in_specs, out_specs=out_specs, check_vma=False)
```

```python
import functools
import math

import jax
import jax.numpy as jnp
import numpy as np
from jax import lax
from jax.experimental import pallas as pl
from jax.experimental.pallas import tpu as pltpu
from jax.sharding import PartitionSpec as P

C = 16
X = 128
YB = 8
HALF = 128
RIM = 64
YC = HALF + RIM
K3 = 3 * YC
VIEWS = 8
F32, BF16 = jnp.float32, jnp.bfloat16
MIB = 1 << 20


def call(kernel, outs, scratch=(), vmem=32, flops=0, moved=0):
    return dict(
        out_shape=outs,
        scratch_shapes=list(scratch),
        compiler_params=pltpu.CompilerParams(vmem_limit_bytes=vmem * MIB),
        cost_estimate=pl.CostEstimate(flops=flops, bytes_accessed=moved, transcendentals=0),
    )


def vmem_spec():
    return pl.BlockSpec(memory_space=pltpu.VMEM)


def hbm_spec():
    return pl.BlockSpec(memory_space=pltpu.HBM)


def smem_spec():
    return pl.BlockSpec(memory_space=pltpu.SMEM)


def band_kernel(taps_ref, base_ref, band_ref):
    lane = lax.broadcasted_iota(jnp.int32, (4 * X, 3 * K3), 1)
    last = YC // C - 1
    for y in range(last + 1):
        kind = 1 if y == 0 else 2 if y == last else 0
        hit = lane == base_ref[:, kind : kind + 1] + y * C
        spread = jnp.where(hit, 1.0, 0.0).astype(BF16)
        rows = jnp.dot(taps_ref[...], spread, preferred_element_type=F32).astype(BF16)
        for n in range(6):
            band_ref[n, y * C : (y + 1) * C, :] = rows[n * C : (n + 1) * C, :]


def band_places():
    a, c, b, i = np.indices((3, 3, 3, C)).reshape(4, -1)
    base = a * K3 + c * YC + (b - 1) * C + i
    base = np.stack([base, np.where(b == 0, -(10**6), base), np.where(b == 2, -(10**6), base)], 1)
    out = np.full((4 * X, 3), -(10**6), np.int32)
    out[: base.shape[0]] = base
    return out


def own_kernel(pieces_ref, grad_hbm, own_ref, sem):
    fetch = pltpu.make_async_copy(grad_hbm, own_ref.at[1], sem)
    fetch.start()
    own_ref[0] = pieces_ref[...].astype(F32).sum(axis=0).astype(BF16)
    fetch.wait()


def facing_kernel(own_ref, far_ref, facing_ref):
    at = pl.multiple_of((1 - lax.axis_index("height")) * RIM, RIM)
    facing_ref[0:2] = own_ref[:, pl.ds(at, RIM), :]
    facing_ref[2:4] = far_ref[:, pl.ds(at, RIM), :]


def parts_kernel(own_ref, far_ref, rim_ref, parts_ref, planes):
    height, view = lax.axis_index("height"), lax.axis_index("view")
    own_at = pl.multiple_of(height * RIM, RIM)
    rim_at = pl.multiple_of((1 - height) * HALF, RIM)
    planes[0:2, pl.ds(own_at, HALF), :] = own_ref[...]
    planes[2:4, pl.ds(own_at, HALF), :] = far_ref[...]
    planes[:, pl.ds(rim_at, RIM), :] = rim_ref[...]
    half = VIEWS // 2
    for v in range(VIEWS):
        away = jnp.abs(v - view)
        parts_ref[v, 0] = planes[jnp.where(away <= half, 0, 2)]
        parts_ref[v, 1] = planes[jnp.where(away == half, 2, jnp.where(away < half, 1, 3))]


def lift_kernel(targets_ref, feats_hbm, weights_hbm, out_ref, feats, weights, total, sems):
    fetch_feats = pltpu.make_async_copy(feats_hbm, feats, sems.at[0])
    fetch_weights = pltpu.make_async_copy(weights_hbm, weights, sems.at[1])
    fetch_feats.start()
    fetch_weights.start()
    total[...] = jnp.zeros_like(total)
    tiles, slots = targets_ref.shape
    fetch_feats.wait()
    fetch_weights.wait()
    for k in range(slots):
        blocks = lax.dot_general(
            feats[...], weights[k], (((1,), (1,)), ((), ())), preferred_element_type=F32
        )
        for t in range(tiles):
            total[targets_ref[t, k]] += blocks[t * C : (t + 1) * C, :]
    out_ref[...] = total[...].astype(BF16).reshape(out_ref.shape)


def camera_kernel(targets_ref, arrived_ref, weights_ref, out_ref, chosen):
    tiles, slots = targets_ref.shape
    for k in range(slots):
        for t in range(tiles):
            target = targets_ref[t, k]
            at = pl.multiple_of(lax.rem(target, YB) * C, C)
            chosen[t * C : (t + 1) * C, k * X : (k + 1) * X] = arrived_ref[
                lax.div(target, YB), pl.ds(at, C), :
            ]
    out_ref[...] = jnp.dot(
        chosen[...], weights_ref[...].reshape(slots * X, X), preferred_element_type=F32
    )


def spread_kernel(scale, sums_ref, weight_ref, bias_ref):
    for q in range(27):
        layer, a, c = q // 9, q // 3 % 3, q % 3
        for b in range(3):
            row = (q // 8 * 3 + b) * C
            block = sums_ref[row : row + C, q % 8 * C : (q % 8 + 1) * C]
            weight_ref[((layer * 3 + a) * 3 + b) * 3 + c] = block * scale
    for layer in range(2):
        lanes = slice((3 + layer) * C, (4 + layer) * C)
        bias_ref[layer : layer + 1, :] = sums_ref[9 * C : 9 * C + 1, lanes] * scale


def silu_and_slope(v):
    s = jax.nn.sigmoid(v)
    return v * s, s * (1.0 + v * (1.0 - s))


def main_kernel(
    arrived_ref,
    band_hbm,
    bias_ref,
    field_ref,
    payload_ref,
    s_lift,
    s_grad,
    s_act1,
    s_act2,
    s_back2,
    s_back1,
    slope1,
    slope2,
    up2,
    band_ref,
    sems,
):
    fetches = [pltpu.make_async_copy(band_hbm.at[n], band_ref.at[n], sems.at[n]) for n in range(6)]
    for n in (0, 3, 1, 4, 5, 2):
        fetches[n].start()
    depth, height, view = (lax.axis_index(n) for n in ("depth", "height", "view"))
    lane = lax.broadcasted_iota(jnp.int32, (YC, X), 1)
    first_lane, last_lane = lane == 0, lane == X - 1
    low = height == 0

    def put(dst, index, plane):
        cols = slice(index * X, (index + 1) * X)
        dst[0:YC, cols] = jnp.where(first_lane, 0.0, pltpu.roll(plane, 1, 1)).astype(BF16)
        dst[YC : 2 * YC, cols] = plane.astype(BF16)
        dst[2 * YC : K3, cols] = jnp.where(last_lane, 0.0, pltpu.roll(plane, X - 1, 1)).astype(
            BF16
        )

    def fetch(offset, kind):
        source = lax.rem(view + offset + VIEWS, VIEWS)
        if offset == -4:
            kind = jnp.where(view < VIEWS // 2, 1, 0)
        if offset == 4:
            kind = jnp.where(view < VIEWS // 2, 0, 1)
        return arrived_ref[source, kind].astype(F32)

    def inside(offset):
        z = depth * VIEWS + view + offset
        return jnp.logical_and(z >= 0, z < lax.axis_size("depth") * VIEWS)

    def masked(offset, plane):
        return jnp.where(inside(offset), plane, 0.0)

    def conv(n, src, start, count):
        taken = [src[:, (start + a) * X : (start + a + count) * X] for a in range(3)]
        out = jnp.dot(band_ref[n], jnp.concatenate(taken, axis=0), preferred_element_type=F32)
        return [out[:, i * X : (i + 1) * X] for i in range(count)]

    own_at = pl.multiple_of(height * RIM, RIM)

    def conv_own(n, src):
        taken = [src[:, a * X : (a + 1) * X] for a in range(3)]
        return jnp.dot(
            band_ref[n, pl.ds(own_at, HALF), :],
            jnp.concatenate(taken, axis=0),
            preferred_element_type=F32,
        )

    def pairs(count):
        return [(i, min(2, count - i)) for i in range(0, count, 2)]

    for i in range(9):
        put(s_lift, i, fetch(i - 4, 0))
    for i in range(7):
        put(s_grad, i, fetch(i - 3, 1))

    bias1, bias2 = bias_ref[0], bias_ref[1]
    fetches[0].wait()
    for i, n in pairs(7):
        for j, pre in enumerate(conv(0, s_lift, i, n)):
            act, slope = silu_and_slope(pre + bias1)
            put(s_act1, i + j, masked(i + j - 3, act))
            if abs(i + j - 3) <= 1:
                slope1[i + j - 2] = slope
    fetches[3].wait()
    for i, n in pairs(5):
        for j, up in enumerate(conv(3, s_grad, i, n)):
            up2[i + j] = up
    fetches[1].wait()
    for i, n in pairs(5):
        for j, pre in enumerate(conv(1, s_act1, i, n)):
            at = i + j
            act, slope = silu_and_slope(pre + bias2)
            back = up2[at] * slope
            put(s_back2, at, masked(at - 2, back))
            if at == 2:
                slope2[...] = back
            if abs(at - 2) <= 1:
                before = s_act1[YC : 2 * YC, (at + 1) * X : (at + 2) * X].astype(F32)
                put(s_act2, at - 1, masked(at - 2, act + before))
    fetches[4].wait()
    for i, n in pairs(3):
        for j, up in enumerate(conv(4, s_back2, i, n)):
            at = i + j
            back = (up2[at + 1] + up) * slope1[at]
            if at == 1:
                slope1[at] = back
            put(s_back1, at, masked(at - 1, back))

    def own_rows(plane):
        return jnp.where(low, plane[:HALF], plane[RIM:])

    fetches[5].wait()
    lift_grad = conv_own(5, s_back1).astype(BF16)
    for v in range(VIEWS):
        payload_ref[v, :HALF, :] = lift_grad
    fetches[2].wait()
    field_ref[...] = conv_own(2, s_act2).astype(BF16)

    wide = (HALF, K3)
    row_y = (lax.broadcasted_iota(jnp.int32, wide, 0) >> 4) + height * (RIM // C)
    col = lax.broadcasted_iota(jnp.int32, wide, 1)
    col_y = (col - jnp.where(col >= 2 * YC, 2 * YC, jnp.where(col >= YC, YC, 0))) >> 4
    bands = [col_y == row_y + (b - 1) for b in range(3)]
    group = lax.broadcasted_iota(jnp.int32, (3 * C, X), 1) // C
    left = lax.broadcasted_iota(jnp.int32, (3 * C, X), 1) < X // 2
    packed = [jnp.zeros((3 * C, X), F32) for _ in range(4)]
    layers = ((s_back1, 1, s_lift, 4), (s_back2, 2, s_act1, 3), (s_grad, 3, s_act2, 1))
    for layer, (g_ref, g_at, v_ref, v_at) in enumerate(layers):
        g = g_ref[pl.ds(YC + own_at, HALF), g_at * X : (g_at + 1) * X]
        for a in range(3):
            at = v_at + a - 1
            products = lax.dot_general(
                g,
                v_ref[:, at * X : (at + 1) * X],
                (((1,), (1,)), ((), ())),
                preferred_element_type=F32,
            )
            by_row = [
                jnp.where(band, products, 0.0).reshape(YB, C, K3).sum(axis=0) for band in bands
            ]
            by_row = jnp.concatenate(by_row, axis=0)
            end = jnp.concatenate([by_row[:, 4 * X :], jnp.zeros((3 * C, X // 2), F32)], axis=1)
            shared = by_row[:, X : 2 * X]
            parts = (
                by_row[:, :X] + jnp.where(left, shared, 0.0),
                by_row[:, 2 * X : 3 * X] + jnp.where(left, 0.0, shared),
                by_row[:, 3 * X : 4 * X] + end,
            )
            for c, part in enumerate(parts):
                for step in (64, 32, 16):
                    part = part + pltpu.roll(part, step, 1)
                q = (layer * 3 + a) * 3 + c
                packed[q // 8] = jnp.where(group == q % 8, part, packed[q // 8])
    for layer, plane in enumerate((slope1[1], slope2[...])):
        sums = jnp.sum(own_rows(plane), axis=1, keepdims=True)
        sums = jnp.broadcast_to(sums, (HALF, X)).reshape(YB, C, X).sum(axis=0)
        out_at = lax.broadcasted_iota(jnp.int32, (C, X), 0)
        to = lax.rem(lax.broadcasted_iota(jnp.int32, (C, X), 1), C)
        sums = jnp.sum(jnp.where(out_at == to, sums, 0.0), axis=0, keepdims=True)
        packed[3] = jnp.where(group == 3 + layer, jnp.broadcast_to(sums, (3 * C, X)), packed[3])
    for v in range(VIEWS):
        start = (v % 2) * 24
        rows = packed[v // 2][start : start + 24]
        high = rows.astype(BF16).astype(F32)
        both = jnp.concatenate([high, rows - high], axis=0)
        payload_ref[v, HALF:, :] = both.astype(BF16)


def main_call(arrived, bands, bias):
    return pl.pallas_call(
        main_kernel,
        in_specs=[vmem_spec(), hbm_spec(), vmem_spec()],
        out_specs=[vmem_spec()] * 2,
        **call(
            main_kernel,
            (
                jax.ShapeDtypeStruct((HALF, X), BF16),
                jax.ShapeDtypeStruct((VIEWS, HALF + 48, X), BF16),
            ),
            [pltpu.VMEM((K3, n * X), BF16) for n in (9, 7, 7, 3, 5, 3)]
            + [
                pltpu.VMEM((3, YC, X), F32),
                pltpu.VMEM((YC, X), F32),
                pltpu.VMEM((5, YC, X), F32),
                pltpu.VMEM((6, YC, 3 * K3), BF16),
                pltpu.SemaphoreType.DMA((6,)),
            ],
            vmem=58,
            flops=10**10,
            moved=10**7,
        ),
    )(arrived, bands, bias)


def flip_swap(weight):
    return jnp.transpose(jnp.flip(weight, (2, 3, 4)), (1, 0, 2, 3, 4))


def for_each(block, axes, groups=None):
    peers = len(groups[0]) if groups else lax.axis_size(axes)
    tiles = jnp.broadcast_to(block[None], (peers, *block.shape))
    return lax.all_to_all(tiles, axes, 0, 0, axis_index_groups=groups, tiled=True)


def body(
    camera_feats,
    footprint_slot_weights,
    tile_bricks,
    tile_rows,
    conv_first,
    conv_second,
    conv_third,
    bias_first,
    bias_second,
    out_grad,
):
    depths, heights, views = (lax.axis_size(n) for n in ("depth", "height", "view"))
    tiles, slots = tile_bricks.shape

    targets = tile_bricks * YB + tile_rows
    partial = pl.pallas_call(
        lift_kernel,
        in_specs=[smem_spec(), hbm_spec(), hbm_spec()],
        out_specs=vmem_spec(),
        **call(
            lift_kernel,
            jax.ShapeDtypeStruct((views, HALF, X), BF16),
            [
                pltpu.VMEM((tiles * C, X), BF16),
                pltpu.VMEM((slots, X, X), BF16),
                pltpu.VMEM((views * YB, C, X), F32),
                pltpu.SemaphoreType.DMA((2,)),
            ],
            vmem=62,
            flops=10**8,
            moved=10**6,
        ),
    )(targets, camera_feats.reshape(tiles * C, X), footprint_slot_weights)
    pieces = lax.all_to_all(partial, "view", 0, 0, tiled=True)

    convs = [conv_first, conv_second, conv_third]
    convs = jnp.stack(convs + [flip_swap(w) for w in reversed(convs)])
    taps = jnp.transpose(convs, (0, 1, 3, 5, 4, 2)).reshape(6 * C, 27 * C)
    taps = jnp.pad(taps, ((0, 0), (0, 4 * X - 27 * C)))
    bands = pl.pallas_call(
        band_kernel,
        in_specs=[vmem_spec()] * 2,
        out_specs=vmem_spec(),
        **call(
            band_kernel,
            jax.ShapeDtypeStruct((6, YC, 3 * K3), BF16),
            flops=10**9,
            moved=7 * 10**6,
        ),
    )(taps, band_places())
    bias = jnp.stack([jnp.tile(b, YC // C) for b in (bias_first, bias_second)])[:, :, None]

    own = pl.pallas_call(
        own_kernel,
        in_specs=[vmem_spec(), hbm_spec()],
        out_specs=vmem_spec(),
        **call(
            own_kernel,
            jax.ShapeDtypeStruct((2, HALF, X), BF16),
            [pltpu.SemaphoreType.DMA],
            vmem=60,
        ),
    )(pieces, out_grad.reshape(HALF, X))
    moves = []
    for d in range(depths):
        for v in range(views):
            to = d + (1 if v >= views // 2 else -1)
            if 0 <= to < depths:
                moves.append((d * views + v, to * views + v))
    far = lax.ppermute(own, ("depth", "view"), moves)
    facing = pl.pallas_call(
        facing_kernel,
        in_specs=[vmem_spec()] * 2,
        out_specs=vmem_spec(),
        **call(facing_kernel, jax.ShapeDtypeStruct((4, RIM, X), BF16)),
    )(own, far)
    rim = lax.ppermute(facing, "height", [(0, 1), (1, 0)])
    parts = pl.pallas_call(
        parts_kernel,
        in_specs=[vmem_spec()] * 3,
        out_specs=vmem_spec(),
        **call(
            parts_kernel,
            jax.ShapeDtypeStruct((VIEWS, 2, YC, X), BF16),
            [pltpu.VMEM((4, YC, X), BF16)],
        ),
    )(own, far, rim)
    arrived = lax.all_to_all(parts, "view", 0, 0, tiled=True)

    field, payload = main_call(arrived, bands, bias)
    arrived = lax.all_to_all(payload, "view", 0, 0, tiled=True)

    sums = arrived[:, HALF:].astype(F32).sum(axis=0)
    sums = sums[:24] + sums[24:]
    run = views
    rings = [list(range(i, i + run)) for i in range(0, depths, run)]
    sums = for_each(sums, "depth", rings).sum(axis=0)
    rings = [
        [(i * run + j) * heights + h for h in range(heights) for i in range(depths // run)]
        for j in range(run)
    ]
    sums = for_each(sums, ("depth", "height"), rings).sum(axis=0)

    camera_grad = pl.pallas_call(
        camera_kernel,
        in_specs=[smem_spec(), vmem_spec(), vmem_spec()],
        out_specs=vmem_spec(),
        **call(
            camera_kernel,
            jax.ShapeDtypeStruct((tiles * C, X), F32),
            [pltpu.VMEM((tiles * C, slots * X), BF16)],
            flops=10**8,
            moved=10**6,
        ),
    )(targets, arrived, footprint_slot_weights)

    sums = for_each(sums, "view").reshape(12 * C, X)
    scale = 1.0 / math.sqrt(YB * X * depths * heights * views)
    weight_grads, bias_gradient_pair = pl.pallas_call(
        functools.partial(spread_kernel, scale),
        in_specs=[vmem_spec()],
        out_specs=[vmem_spec()] * 2,
        **call(
            spread_kernel,
            (jax.ShapeDtypeStruct((81, C, C), F32), jax.ShapeDtypeStruct((2, C), F32)),
        ),
    )(sums)
    weight_grads = jnp.transpose(weight_grads.reshape(3, 3, 3, 3, C, C), (0, 4, 5, 1, 2, 3))
    return (
        field.reshape(1, YB, C, X),
        camera_grad.reshape(tiles, C, X),
        weight_grads,
        bias_gradient_pair,
    )


def solution(mesh):
    in_specs = (
        P(("depth", "height", "view"), None, None),
        P(),
        P(("depth", "height", "view"), None),
        P(("depth", "height", "view"), None),
        P(),
        P(),
        P(),
        P(),
        P(),
        P(("depth", "view"), "height", None, None),
    )
    out_specs = (
        P(("depth", "view"), "height", None, None),
        P(("depth", "height", "view"), None, None),
        P(),
        P(),
    )
    return jax.shard_map(body, mesh=mesh, in_specs=in_specs, out_specs=out_specs, check_vma=False)
```

```python
import functools
import math

import jax
import jax.numpy as jnp
import numpy as np
from jax import lax
from jax.experimental import pallas as pl
from jax.experimental.pallas import tpu as pltpu
from jax.sharding import PartitionSpec as P

C = 16
X = 128
YB = 8
HALF = 128
RIM = 64
YC = HALF + RIM
K3 = 3 * YC
VIEWS = 8
F32, BF16 = jnp.float32, jnp.bfloat16
MIB = 1 << 20


def call(kernel, outs, scratch=(), vmem=32, flops=0, moved=0):
    return dict(
        out_shape=outs,
        scratch_shapes=list(scratch),
        compiler_params=pltpu.CompilerParams(vmem_limit_bytes=vmem * MIB),
        cost_estimate=pl.CostEstimate(flops=flops, bytes_accessed=moved, transcendentals=0),
    )


def vmem_spec():
    return pl.BlockSpec(memory_space=pltpu.VMEM)


def hbm_spec():
    return pl.BlockSpec(memory_space=pltpu.HBM)


def smem_spec():
    return pl.BlockSpec(memory_space=pltpu.SMEM)


def band_kernel(taps_ref, base_ref, band_ref):
    lane = lax.broadcasted_iota(jnp.int32, (4 * X, 3 * K3), 1)
    last = YC // C - 1
    for y in range(last + 1):
        kind = 1 if y == 0 else 2 if y == last else 0
        hit = lane == base_ref[:, kind : kind + 1] + y * C
        spread = jnp.where(hit, 1.0, 0.0).astype(BF16)
        rows = jnp.dot(taps_ref[...], spread, preferred_element_type=F32).astype(BF16)
        for n in range(6):
            band_ref[n, y * C : (y + 1) * C, :] = rows[n * C : (n + 1) * C, :]


def band_places():
    a, c, b, i = np.indices((3, 3, 3, C)).reshape(4, -1)
    base = a * K3 + c * YC + (b - 1) * C + i
    base = np.stack([base, np.where(b == 0, -(10**6), base), np.where(b == 2, -(10**6), base)], 1)
    out = np.full((4 * X, 3), -(10**6), np.int32)
    out[: base.shape[0]] = base
    return out


def own_kernel(pieces_ref, grad_ref, own_ref):
    own_ref[0] = pieces_ref[...].astype(F32).sum(axis=0).astype(BF16)
    own_ref[1] = grad_ref[...]


def facing_kernel(own_ref, far_ref, facing_ref):
    at = pl.multiple_of((1 - lax.axis_index("height")) * RIM, RIM)
    facing_ref[0:2] = own_ref[:, pl.ds(at, RIM), :]
    facing_ref[2:4] = far_ref[:, pl.ds(at, RIM), :]


def parts_kernel(own_ref, far_ref, rim_ref, parts_ref, planes):
    height, view = lax.axis_index("height"), lax.axis_index("view")
    own_at = pl.multiple_of(height * RIM, RIM)
    rim_at = pl.multiple_of((1 - height) * HALF, RIM)
    planes[0:2, pl.ds(own_at, HALF), :] = own_ref[...]
    planes[2:4, pl.ds(own_at, HALF), :] = far_ref[...]
    planes[:, pl.ds(rim_at, RIM), :] = rim_ref[...]
    half = VIEWS // 2
    for v in range(VIEWS):
        away = jnp.abs(v - view)
        parts_ref[v, 0] = planes[jnp.where(away <= half, 0, 2)]
        parts_ref[v, 1] = planes[jnp.where(away == half, 2, jnp.where(away < half, 1, 3))]


def lift_kernel(bricks_ref, rows_ref, feats_hbm, weights_hbm, out_ref, feats, weights, total, sems):
    fetch_feats = pltpu.make_async_copy(feats_hbm, feats, sems.at[0])
    fetch_weights = pltpu.make_async_copy(weights_hbm, weights, sems.at[1])
    fetch_feats.start()
    fetch_weights.start()
    total[...] = jnp.zeros_like(total)
    tiles, slots = bricks_ref.shape
    fetch_feats.wait()
    fetch_weights.wait()
    for k in range(slots):
        blocks = lax.dot_general(
            feats[...], weights[k], (((1,), (1,)), ((), ())), preferred_element_type=F32
        )
        for t in range(tiles):
            total[bricks_ref[t, k] * YB + rows_ref[t, k]] += blocks[t * C : (t + 1) * C, :]
    out_ref[...] = total[...].astype(BF16).reshape(out_ref.shape)


def camera_kernel(bricks_ref, rows_ref, arrived_ref, weights_ref, out_ref, chosen):
    tiles, slots = bricks_ref.shape
    for k in range(slots):
        for t in range(tiles):
            at = pl.multiple_of(rows_ref[t, k] * C, C)
            chosen[t * C : (t + 1) * C, k * X : (k + 1) * X] = arrived_ref[
                bricks_ref[t, k], pl.ds(at, C), :
            ]
    out_ref[...] = jnp.dot(
        chosen[...], weights_ref[...].reshape(slots * X, X), preferred_element_type=F32
    )


def first_sum_kernel(arrived_ref, out_ref):
    sums = arrived_ref[:, HALF:, :].astype(F32).sum(axis=0)
    out_ref[...] = jnp.broadcast_to((sums[:24] + sums[24:])[None], out_ref.shape)


def next_sum_kernel(arrived_ref, out_ref):
    out_ref[...] = jnp.broadcast_to(arrived_ref[...].sum(axis=0, keepdims=True), out_ref.shape)


def spread_kernel(scale, sums_ref, weight_ref, bias_ref):
    for q in range(27):
        layer, a, c = q // 9, q // 3 % 3, q % 3
        for b in range(3):
            row = (q // 8 * 3 + b) * C
            block = sums_ref[row : row + C, q % 8 * C : (q % 8 + 1) * C]
            weight_ref[((layer * 3 + a) * 3 + b) * 3 + c] = block * scale
    for layer in range(2):
        lanes = slice((3 + layer) * C, (4 + layer) * C)
        bias_ref[layer : layer + 1, :] = sums_ref[9 * C : 9 * C + 1, lanes] * scale


def silu_and_slope(v):
    s = jax.nn.sigmoid(v)
    return v * s, s * (1.0 + v * (1.0 - s))


def main_kernel(
    arrived_ref,
    band_hbm,
    bias_ref,
    field_ref,
    payload_ref,
    s_lift,
    s_grad,
    s_act1,
    s_act2,
    s_back2,
    s_back1,
    slope1,
    slope2,
    up2,
    band_ref,
    sems,
):
    fetches = [pltpu.make_async_copy(band_hbm.at[n], band_ref.at[n], sems.at[n]) for n in range(6)]
    for n in (0, 3, 1, 4, 5, 2):
        fetches[n].start()
    depth, height, view = (lax.axis_index(n) for n in ("depth", "height", "view"))
    lane = lax.broadcasted_iota(jnp.int32, (YC, X), 1)
    first_lane, last_lane = lane == 0, lane == X - 1
    low = height == 0

    def put(dst, index, plane):
        cols = slice(index * X, (index + 1) * X)
        dst[0:YC, cols] = jnp.where(first_lane, 0.0, pltpu.roll(plane, 1, 1)).astype(BF16)
        dst[YC : 2 * YC, cols] = plane.astype(BF16)
        dst[2 * YC : K3, cols] = jnp.where(last_lane, 0.0, pltpu.roll(plane, X - 1, 1)).astype(
            BF16
        )

    def fetch(offset, kind):
        source = lax.rem(view + offset + VIEWS, VIEWS)
        if offset == -4:
            kind = jnp.where(view < VIEWS // 2, 1, 0)
        if offset == 4:
            kind = jnp.where(view < VIEWS // 2, 0, 1)
        return arrived_ref[source, kind].astype(F32)

    def inside(offset):
        z = depth * VIEWS + view + offset
        return jnp.logical_and(z >= 0, z < lax.axis_size("depth") * VIEWS)

    def masked(offset, plane):
        return jnp.where(inside(offset), plane, 0.0)

    def conv(n, src, start, count):
        taken = [src[:, (start + a) * X : (start + a + count) * X] for a in range(3)]
        out = jnp.dot(band_ref[n], jnp.concatenate(taken, axis=0), preferred_element_type=F32)
        return [out[:, i * X : (i + 1) * X] for i in range(count)]

    own_at = pl.multiple_of(height * RIM, RIM)

    def conv_own(n, src):
        taken = [src[:, a * X : (a + 1) * X] for a in range(3)]
        return jnp.dot(
            band_ref[n, pl.ds(own_at, HALF), :],
            jnp.concatenate(taken, axis=0),
            preferred_element_type=F32,
        )

    def pairs(count):
        return [(i, min(2, count - i)) for i in range(0, count, 2)]

    for i in range(9):
        put(s_lift, i, fetch(i - 4, 0))
    for i in range(7):
        put(s_grad, i, fetch(i - 3, 1))

    bias1, bias2 = bias_ref[0], bias_ref[1]
    fetches[0].wait()
    for i, n in pairs(7):
        for j, pre in enumerate(conv(0, s_lift, i, n)):
            act, slope = silu_and_slope(pre + bias1)
            put(s_act1, i + j, masked(i + j - 3, act))
            if abs(i + j - 3) <= 1:
                slope1[i + j - 2] = slope
    fetches[3].wait()
    for i, n in pairs(5):
        for j, up in enumerate(conv(3, s_grad, i, n)):
            up2[i + j] = up
    fetches[1].wait()
    for i, n in pairs(5):
        for j, pre in enumerate(conv(1, s_act1, i, n)):
            at = i + j
            act, slope = silu_and_slope(pre + bias2)
            back = up2[at] * slope
            put(s_back2, at, masked(at - 2, back))
            if at == 2:
                slope2[...] = back
            if abs(at - 2) <= 1:
                before = s_act1[YC : 2 * YC, (at + 1) * X : (at + 2) * X].astype(F32)
                put(s_act2, at - 1, masked(at - 2, act + before))
    fetches[4].wait()
    for i, n in pairs(3):
        for j, up in enumerate(conv(4, s_back2, i, n)):
            at = i + j
            back = (up2[at + 1] + up) * slope1[at]
            if at == 1:
                slope1[at] = back
            put(s_back1, at, masked(at - 1, back))

    def own_rows(plane):
        return jnp.where(low, plane[:HALF], plane[RIM:])

    fetches[5].wait()
    lift_grad = conv_own(5, s_back1).astype(BF16)
    for v in range(VIEWS):
        payload_ref[v, :HALF, :] = lift_grad
    fetches[2].wait()
    field_ref[...] = conv_own(2, s_act2).astype(BF16)

    wide = (HALF, K3)
    row_y = (lax.broadcasted_iota(jnp.int32, wide, 0) >> 4) + height * (RIM // C)
    col = lax.broadcasted_iota(jnp.int32, wide, 1)
    col_y = (col - jnp.where(col >= 2 * YC, 2 * YC, jnp.where(col >= YC, YC, 0))) >> 4
    bands = [col_y == row_y + (b - 1) for b in range(3)]
    group = lax.broadcasted_iota(jnp.int32, (3 * C, X), 1) // C
    left = lax.broadcasted_iota(jnp.int32, (3 * C, X), 1) < X // 2
    packed = [jnp.zeros((3 * C, X), F32) for _ in range(4)]
    layers = ((s_back1, 1, s_lift, 4), (s_back2, 2, s_act1, 3), (s_grad, 3, s_act2, 1))
    for layer, (g_ref, g_at, v_ref, v_at) in enumerate(layers):
        g = g_ref[pl.ds(YC + own_at, HALF), g_at * X : (g_at + 1) * X]
        for a in range(3):
            at = v_at + a - 1
            products = lax.dot_general(
                g,
                v_ref[:, at * X : (at + 1) * X],
                (((1,), (1,)), ((), ())),
                preferred_element_type=F32,
            )
            by_row = [
                jnp.where(band, products, 0.0).reshape(YB, C, K3).sum(axis=0) for band in bands
            ]
            by_row = jnp.concatenate(by_row, axis=0)
            end = jnp.concatenate([by_row[:, 4 * X :], jnp.zeros((3 * C, X // 2), F32)], axis=1)
            shared = by_row[:, X : 2 * X]
            parts = (
                by_row[:, :X] + jnp.where(left, shared, 0.0),
                by_row[:, 2 * X : 3 * X] + jnp.where(left, 0.0, shared),
                by_row[:, 3 * X : 4 * X] + end,
            )
            for c, part in enumerate(parts):
                for step in (64, 32, 16):
                    part = part + pltpu.roll(part, step, 1)
                q = (layer * 3 + a) * 3 + c
                packed[q // 8] = jnp.where(group == q % 8, part, packed[q // 8])
    for layer, plane in enumerate((slope1[1], slope2[...])):
        sums = jnp.sum(own_rows(plane), axis=1, keepdims=True)
        sums = jnp.broadcast_to(sums, (HALF, X)).reshape(YB, C, X).sum(axis=0)
        out_at = lax.broadcasted_iota(jnp.int32, (C, X), 0)
        to = lax.rem(lax.broadcasted_iota(jnp.int32, (C, X), 1), C)
        sums = jnp.sum(jnp.where(out_at == to, sums, 0.0), axis=0, keepdims=True)
        packed[3] = jnp.where(group == 3 + layer, jnp.broadcast_to(sums, (3 * C, X)), packed[3])
    for v in range(VIEWS):
        start = (v % 2) * 24
        rows = packed[v // 2][start : start + 24]
        high = rows.astype(BF16).astype(F32)
        both = jnp.concatenate([high, rows - high], axis=0)
        payload_ref[v, HALF:, :] = both.astype(BF16)


def main_call(arrived, bands, bias):
    return pl.pallas_call(
        main_kernel,
        in_specs=[vmem_spec(), hbm_spec(), vmem_spec()],
        out_specs=[vmem_spec()] * 2,
        **call(
            main_kernel,
            (
                jax.ShapeDtypeStruct((HALF, X), BF16),
                jax.ShapeDtypeStruct((VIEWS, HALF + 48, X), BF16),
            ),
            [pltpu.VMEM((K3, n * X), BF16) for n in (9, 7, 7, 3, 5, 3)]
            + [
                pltpu.VMEM((3, YC, X), F32),
                pltpu.VMEM((YC, X), F32),
                pltpu.VMEM((5, YC, X), F32),
                pltpu.VMEM((6, YC, 3 * K3), BF16),
                pltpu.SemaphoreType.DMA((6,)),
            ],
            vmem=52,
            flops=10**10,
            moved=10**7,
        ),
    )(arrived, bands, bias)


def flip_swap(weight):
    return jnp.transpose(jnp.flip(weight, (2, 3, 4)), (1, 0, 2, 3, 4))


def for_each_sum(kernel, arrived):
    return pl.pallas_call(
        kernel,
        in_specs=[vmem_spec()],
        out_specs=vmem_spec(),
        **call(kernel, jax.ShapeDtypeStruct((VIEWS, 24, X), F32), vmem=16),
    )(arrived)


def body(
    camera_feats,
    footprint_slot_weights,
    tile_bricks,
    tile_rows,
    conv_first,
    conv_second,
    conv_third,
    bias_first,
    bias_second,
    out_grad,
):
    depths, heights, views = (lax.axis_size(n) for n in ("depth", "height", "view"))
    tiles, slots = tile_bricks.shape

    partial = pl.pallas_call(
        lift_kernel,
        in_specs=[smem_spec(), smem_spec(), hbm_spec(), hbm_spec()],
        out_specs=vmem_spec(),
        **call(
            lift_kernel,
            jax.ShapeDtypeStruct((views, HALF, X), BF16),
            [
                pltpu.VMEM((tiles * C, X), BF16),
                pltpu.VMEM((slots, X, X), BF16),
                pltpu.VMEM((views * YB, C, X), F32),
                pltpu.SemaphoreType.DMA((2,)),
            ],
            vmem=62,
            flops=10**8,
            moved=10**6,
        ),
    )(tile_bricks, tile_rows, camera_feats.reshape(tiles * C, X), footprint_slot_weights)
    pieces = lax.all_to_all(partial, "view", 0, 0, tiled=True)

    convs = [conv_first, conv_second, conv_third]
    convs = jnp.stack(convs + [flip_swap(w) for w in reversed(convs)])
    taps = jnp.transpose(convs, (0, 1, 3, 5, 4, 2)).reshape(6 * C, 27 * C)
    taps = jnp.pad(taps, ((0, 0), (0, 4 * X - 27 * C)))
    bands = pl.pallas_call(
        band_kernel,
        in_specs=[vmem_spec()] * 2,
        out_specs=vmem_spec(),
        **call(
            band_kernel,
            jax.ShapeDtypeStruct((6, YC, 3 * K3), BF16),
            flops=10**9,
            moved=7 * 10**6,
        ),
    )(taps, band_places())
    bias = jnp.stack([jnp.tile(b, YC // C) for b in (bias_first, bias_second)])[:, :, None]

    own = pl.pallas_call(
        own_kernel,
        in_specs=[vmem_spec()] * 2,
        out_specs=vmem_spec(),
        **call(own_kernel, jax.ShapeDtypeStruct((2, HALF, X), BF16), vmem=16),
    )(pieces, out_grad.reshape(HALF, X))
    moves = []
    for d in range(depths):
        for v in range(views):
            to = d + (1 if v >= views // 2 else -1)
            if 0 <= to < depths:
                moves.append((d * views + v, to * views + v))
    far = lax.ppermute(own, ("depth", "view"), moves)
    facing = pl.pallas_call(
        facing_kernel,
        in_specs=[vmem_spec()] * 2,
        out_specs=vmem_spec(),
        **call(facing_kernel, jax.ShapeDtypeStruct((4, RIM, X), BF16)),
    )(own, far)
    rim = lax.ppermute(facing, "height", [(0, 1), (1, 0)])
    parts = pl.pallas_call(
        parts_kernel,
        in_specs=[vmem_spec()] * 3,
        out_specs=vmem_spec(),
        **call(
            parts_kernel,
            jax.ShapeDtypeStruct((VIEWS, 2, YC, X), BF16),
            [pltpu.VMEM((4, YC, X), BF16)],
        ),
    )(own, far, rim)
    arrived = lax.all_to_all(parts, "view", 0, 0, tiled=True)

    field, payload = main_call(arrived, bands, bias)
    arrived = lax.all_to_all(payload, "view", 0, 0, tiled=True)

    run = views
    sums = for_each_sum(first_sum_kernel, arrived)
    rings = [list(range(i, i + run)) for i in range(0, depths, run)]
    sums = lax.all_to_all(sums, "depth", 0, 0, axis_index_groups=rings, tiled=True)
    sums = for_each_sum(next_sum_kernel, sums)
    rings = [
        [(i * run + j) * heights + h for h in range(heights) for i in range(depths // run)]
        for j in range(run)
    ]
    sums = lax.all_to_all(
        sums, ("depth", "height"), 0, 0, axis_index_groups=rings, tiled=True
    )
    sums = for_each_sum(next_sum_kernel, sums)

    camera_grad = pl.pallas_call(
        camera_kernel,
        in_specs=[smem_spec(), smem_spec(), vmem_spec(), vmem_spec()],
        out_specs=vmem_spec(),
        **call(
            camera_kernel,
            jax.ShapeDtypeStruct((tiles * C, X), F32),
            [pltpu.VMEM((tiles * C, slots * X), BF16)],
            flops=10**8,
            moved=10**6,
        ),
    )(tile_bricks, tile_rows, arrived, footprint_slot_weights)

    sums = lax.all_to_all(sums, "view", 0, 0, tiled=True).reshape(12 * C, X)
    scale = 1.0 / math.sqrt(YB * X * depths * heights * views)
    weight_grads, bias_gradient_pair = pl.pallas_call(
        functools.partial(spread_kernel, scale),
        in_specs=[vmem_spec()],
        out_specs=[vmem_spec()] * 2,
        **call(
            spread_kernel,
            (jax.ShapeDtypeStruct((81, C, C), F32), jax.ShapeDtypeStruct((2, C), F32)),
        ),
    )(sums)
    weight_grads = jnp.transpose(weight_grads.reshape(3, 3, 3, 3, C, C), (0, 4, 5, 1, 2, 3))
    return (
        field.reshape(1, YB, C, X),
        camera_grad.reshape(tiles, C, X),
        weight_grads,
        bias_gradient_pair,
    )


def solution(mesh):
    in_specs = (
        P(("depth", "height", "view"), None, None),
        P(),
        P(("depth", "height", "view"), None),
        P(("depth", "height", "view"), None),
        P(),
        P(),
        P(),
        P(),
        P(),
        P(("depth", "view"), "height", None, None),
    )
    out_specs = (
        P(("depth", "view"), "height", None, None),
        P(("depth", "height", "view"), None, None),
        P(),
        P(),
    )
    return jax.shard_map(body, mesh=mesh, in_specs=in_specs, out_specs=out_specs, check_vma=False)
```

```python
import functools
import math

import jax
import jax.numpy as jnp
import numpy as np
from jax import lax
from jax.experimental import pallas as pl
from jax.experimental.pallas import tpu as pltpu
from jax.sharding import PartitionSpec as P

C = 16
X = 128
YB = 8
HALF = 128
RIM = 64
YC = HALF + RIM
K3 = 3 * YC
VIEWS = 8
F32, BF16 = jnp.float32, jnp.bfloat16
MIB = 1 << 20


def call(kernel, outs, scratch=(), vmem=32, flops=0, moved=0):
    return dict(
        out_shape=outs,
        scratch_shapes=list(scratch),
        compiler_params=pltpu.CompilerParams(vmem_limit_bytes=vmem * MIB),
        cost_estimate=pl.CostEstimate(flops=flops, bytes_accessed=moved, transcendentals=0),
    )


def vmem_spec():
    return pl.BlockSpec(memory_space=pltpu.VMEM)


def hbm_spec():
    return pl.BlockSpec(memory_space=pltpu.HBM)


def smem_spec():
    return pl.BlockSpec(memory_space=pltpu.SMEM)


def block_kernel(taps_ref, place_ref, block_ref):
    lane = lax.broadcasted_iota(jnp.int32, (4 * X, 14 * X), 1)
    spread = jnp.where(lane == place_ref[...], 1.0, 0.0).astype(BF16)
    block_ref[...] = jnp.dot(taps_ref[...], spread, preferred_element_type=F32).astype(BF16)


def block_places():
    a, c, b, i = np.indices((3, 3, 3, C)).reshape(4, -1)
    out = np.full((4 * X, 1), -1, np.int32)
    out[: a.size, 0] = a * K3 + c * YC + b * C + i
    return out


def own_kernel(pieces_ref, grad_ref, own_ref):
    own_ref[0] = pieces_ref[...].astype(F32).sum(axis=0).astype(BF16)
    own_ref[1] = grad_ref[...]


def facing_kernel(own_ref, far_ref, facing_ref):
    at = pl.multiple_of((1 - lax.axis_index("height")) * RIM, RIM)
    facing_ref[0:2] = own_ref[:, pl.ds(at, RIM), :]
    facing_ref[2:4] = far_ref[:, pl.ds(at, RIM), :]


def parts_kernel(own_ref, far_ref, rim_ref, parts_ref, planes):
    height, view = lax.axis_index("height"), lax.axis_index("view")
    own_at = pl.multiple_of(height * RIM, RIM)
    rim_at = pl.multiple_of((1 - height) * HALF, RIM)
    planes[0:2, pl.ds(own_at, HALF), :] = own_ref[...]
    planes[2:4, pl.ds(own_at, HALF), :] = far_ref[...]
    planes[:, pl.ds(rim_at, RIM), :] = rim_ref[...]
    half = VIEWS // 2
    for v in range(VIEWS):
        away = jnp.abs(v - view)
        parts_ref[v, 0] = planes[jnp.where(away <= half, 0, 2)]
        parts_ref[v, 1] = planes[jnp.where(away == half, 2, jnp.where(away < half, 1, 3))]


def lift_kernel(bricks_ref, rows_ref, feats_hbm, weights_hbm, out_ref, feats, weights, total, sems):
    fetch_feats = pltpu.make_async_copy(feats_hbm, feats, sems.at[0])
    fetch_weights = pltpu.make_async_copy(weights_hbm, weights, sems.at[1])
    fetch_feats.start()
    fetch_weights.start()
    total[...] = jnp.zeros_like(total)
    tiles, slots = bricks_ref.shape
    fetch_feats.wait()
    fetch_weights.wait()
    for k in range(slots):
        blocks = lax.dot_general(
            feats[...], weights[k], (((1,), (1,)), ((), ())), preferred_element_type=F32
        )
        for t in range(tiles):
            total[bricks_ref[t, k] * YB + rows_ref[t, k]] += blocks[t * C : (t + 1) * C, :]
    out_ref[...] = total[...].astype(BF16).reshape(out_ref.shape)


def camera_kernel(bricks_ref, rows_ref, arrived_ref, weights_ref, out_ref, chosen):
    tiles, slots = bricks_ref.shape
    for k in range(slots):
        for t in range(tiles):
            at = pl.multiple_of(rows_ref[t, k] * C, C)
            chosen[t * C : (t + 1) * C, k * X : (k + 1) * X] = arrived_ref[
                bricks_ref[t, k], pl.ds(at, C), :
            ]
    out_ref[...] = jnp.dot(
        chosen[...], weights_ref[...].reshape(slots * X, X), preferred_element_type=F32
    )


def first_sum_kernel(arrived_ref, out_ref):
    sums = arrived_ref[:, HALF:, :].astype(F32).sum(axis=0)
    sums = sums[:24] + sums[24:]
    lost = sums - sums.astype(BF16).astype(F32)
    group = lax.broadcasted_iota(jnp.int32, sums.shape, 1) >> 4
    spare = jnp.logical_and(group >= 5, lax.axis_index("view") >= VIEWS - 2)
    sums = jnp.where(spare, pltpu.roll(lost, 2 * C, 1), sums).astype(BF16)
    out_ref[...] = jnp.broadcast_to(sums[None], out_ref.shape)


def next_sum_kernel(arrived_ref, out_ref):
    sums = arrived_ref[...].astype(F32).sum(axis=0, keepdims=True)
    out_ref[...] = jnp.broadcast_to(sums, out_ref.shape)


def spread_kernel(scale, sums_ref, weight_ref, bias_ref):
    for q in range(27):
        layer, a, c = q // 9, q // 3 % 3, q % 3
        for b in range(3):
            row = (q // 8 * 3 + b) * C
            block = sums_ref[row : row + C, q % 8 * C : (q % 8 + 1) * C]
            weight_ref[((layer * 3 + a) * 3 + b) * 3 + c] = block * scale
    for layer in range(2):
        lanes, lost = (slice((n + layer) * C, (n + 1 + layer) * C) for n in (3, 5))
        row = sums_ref[9 * C : 9 * C + 1, :]
        bias_ref[layer : layer + 1, :] = (row[:, lanes] + row[:, lost]) * scale


def silu_and_slope(v):
    s = jax.nn.sigmoid(v)
    return v * s, s * (1.0 + v * (1.0 - s))


def main_kernel(
    arrived_ref,
    block_hbm,
    bias_ref,
    field_ref,
    payload_ref,
    s_lift,
    s_grad,
    s_act1,
    s_act2,
    s_back2,
    s_back1,
    slope1,
    slope2,
    up2,
    band_ref,
    block_ref,
    sem,
):
    fetch_blocks = pltpu.make_async_copy(block_hbm, block_ref, sem)
    fetch_blocks.start()
    depth, height, view = (lax.axis_index(n) for n in ("depth", "height", "view"))
    lane = lax.broadcasted_iota(jnp.int32, (YC, X), 1)
    first_lane, last_lane = lane == 0, lane == X - 1
    low = height == 0

    def put(dst, index, plane):
        cols = slice(index * X, (index + 1) * X)
        dst[0:YC, cols] = jnp.where(first_lane, 0.0, pltpu.roll(plane, 1, 1)).astype(BF16)
        dst[YC : 2 * YC, cols] = plane.astype(BF16)
        dst[2 * YC : K3, cols] = jnp.where(last_lane, 0.0, pltpu.roll(plane, X - 1, 1)).astype(
            BF16
        )

    def fetch(offset, kind):
        source = lax.rem(view + offset + VIEWS, VIEWS)
        if offset == -4:
            kind = jnp.where(view < VIEWS // 2, 1, 0)
        if offset == 4:
            kind = jnp.where(view < VIEWS // 2, 0, 1)
        return arrived_ref[source, kind].astype(F32)

    def inside(offset):
        z = depth * VIEWS + view + offset
        return jnp.logical_and(z >= 0, z < lax.axis_size("depth") * VIEWS)

    def masked(offset, plane):
        return jnp.where(inside(offset), plane, 0.0)

    def conv(n, src, start, count):
        taken = [src[:, (start + a) * X : (start + a + count) * X] for a in range(3)]
        out = jnp.dot(band_ref[n], jnp.concatenate(taken, axis=0), preferred_element_type=F32)
        return [out[:, i * X : (i + 1) * X] for i in range(count)]

    own_at = pl.multiple_of(height * RIM, RIM)

    def conv_own(n, src):
        taken = [src[:, a * X : (a + 1) * X] for a in range(3)]
        return jnp.dot(
            band_ref[n, pl.ds(own_at, HALF), :],
            jnp.concatenate(taken, axis=0),
            preferred_element_type=F32,
        )

    def pairs(count):
        return [(i, min(2, count - i)) for i in range(0, count, 2)]

    for i in range(9):
        put(s_lift, i, fetch(i - 4, 0))
    for i in range(7):
        put(s_grad, i, fetch(i - 3, 1))

    fetch_blocks.wait()
    at = lax.broadcasted_iota(jnp.int32, (C, 14 * X), 1)
    below, above = at < 0, at < 0
    for w in range(9):
        start = w * YC
        below = jnp.logical_or(below, jnp.logical_and(at >= start, at < start + C))
        above = jnp.logical_or(above, jnp.logical_and(at >= start + 2 * C, at < start + 3 * C))
    for n in (0, 3, 1, 4, 5, 2):
        block = block_ref[n * C : (n + 1) * C, :].astype(F32)
        for y in range(YC // C):
            rows = block
            if y == 0:
                rows = jnp.where(below, 0.0, block)
            if y == YC // C - 1:
                rows = jnp.where(above, 0.0, block)
            if y != 1:
                rows = pltpu.roll(rows, (y - 1) * C % (14 * X), 1)
            band_ref[n, y * C : (y + 1) * C, :] = rows[:, : 3 * K3].astype(BF16)

    bias1, bias2 = bias_ref[0], bias_ref[1]
    for i, n in pairs(7):
        for j, pre in enumerate(conv(0, s_lift, i, n)):
            act, slope = silu_and_slope(pre + bias1)
            put(s_act1, i + j, masked(i + j - 3, act))
            if abs(i + j - 3) <= 1:
                slope1[i + j - 2] = slope
    for i, n in pairs(5):
        for j, up in enumerate(conv(3, s_grad, i, n)):
            up2[i + j] = up
    for i, n in pairs(5):
        for j, pre in enumerate(conv(1, s_act1, i, n)):
            at = i + j
            act, slope = silu_and_slope(pre + bias2)
            back = up2[at] * slope
            put(s_back2, at, masked(at - 2, back))
            if at == 2:
                slope2[...] = back
            if abs(at - 2) <= 1:
                before = s_act1[YC : 2 * YC, (at + 1) * X : (at + 2) * X].astype(F32)
                put(s_act2, at - 1, masked(at - 2, act + before))
    for i, n in pairs(3):
        for j, up in enumerate(conv(4, s_back2, i, n)):
            at = i + j
            back = (up2[at + 1] + up) * slope1[at]
            if at == 1:
                slope1[at] = back
            put(s_back1, at, masked(at - 1, back))

    def own_rows(plane):
        return jnp.where(low, plane[:HALF], plane[RIM:])

    lift_grad = conv_own(5, s_back1).astype(BF16)
    for v in range(VIEWS):
        payload_ref[v, :HALF, :] = lift_grad
    field_ref[...] = conv_own(2, s_act2).astype(BF16)

    wide = (HALF, K3)
    row_y = (lax.broadcasted_iota(jnp.int32, wide, 0) >> 4) + height * (RIM // C)
    col = lax.broadcasted_iota(jnp.int32, wide, 1)
    col_y = (col - jnp.where(col >= 2 * YC, 2 * YC, jnp.where(col >= YC, YC, 0))) >> 4
    bands = [col_y == row_y + (b - 1) for b in range(3)]
    group = lax.broadcasted_iota(jnp.int32, (3 * C, X), 1) // C
    left = lax.broadcasted_iota(jnp.int32, (3 * C, X), 1) < X // 2
    packed = [jnp.zeros((3 * C, X), F32) for _ in range(4)]
    layers = ((s_back1, 1, s_lift, 4), (s_back2, 2, s_act1, 3), (s_grad, 3, s_act2, 1))
    for layer, (g_ref, g_at, v_ref, v_at) in enumerate(layers):
        g = g_ref[pl.ds(YC + own_at, HALF), g_at * X : (g_at + 1) * X]
        for a in range(3):
            at = v_at + a - 1
            products = lax.dot_general(
                g,
                v_ref[:, at * X : (at + 1) * X],
                (((1,), (1,)), ((), ())),
                preferred_element_type=F32,
            )
            by_row = [
                jnp.where(band, products, 0.0).reshape(YB, C, K3).sum(axis=0) for band in bands
            ]
            by_row = jnp.concatenate(by_row, axis=0)
            end = jnp.concatenate([by_row[:, 4 * X :], jnp.zeros((3 * C, X // 2), F32)], axis=1)
            shared = by_row[:, X : 2 * X]
            parts = (
                by_row[:, :X] + jnp.where(left, shared, 0.0),
                by_row[:, 2 * X : 3 * X] + jnp.where(left, 0.0, shared),
                by_row[:, 3 * X : 4 * X] + end,
            )
            for c, part in enumerate(parts):
                for step in (64, 32, 16):
                    part = part + pltpu.roll(part, step, 1)
                q = (layer * 3 + a) * 3 + c
                packed[q // 8] = jnp.where(group == q % 8, part, packed[q // 8])
    for layer, plane in enumerate((slope1[1], slope2[...])):
        sums = jnp.sum(own_rows(plane), axis=1, keepdims=True)
        sums = jnp.broadcast_to(sums, (HALF, X)).reshape(YB, C, X).sum(axis=0)
        out_at = lax.broadcasted_iota(jnp.int32, (C, X), 0)
        to = lax.rem(lax.broadcasted_iota(jnp.int32, (C, X), 1), C)
        sums = jnp.sum(jnp.where(out_at == to, sums, 0.0), axis=0, keepdims=True)
        packed[3] = jnp.where(group == 3 + layer, jnp.broadcast_to(sums, (3 * C, X)), packed[3])
    for v in range(VIEWS):
        start = (v % 2) * 24
        rows = packed[v // 2][start : start + 24]
        high = rows.astype(BF16).astype(F32)
        both = jnp.concatenate([high, rows - high], axis=0)
        payload_ref[v, HALF:, :] = both.astype(BF16)


def main_call(arrived, blocks, bias):
    return pl.pallas_call(
        main_kernel,
        in_specs=[vmem_spec(), hbm_spec(), vmem_spec()],
        out_specs=[vmem_spec()] * 2,
        **call(
            main_kernel,
            (
                jax.ShapeDtypeStruct((HALF, X), BF16),
                jax.ShapeDtypeStruct((VIEWS, HALF + 48, X), BF16),
            ),
            [pltpu.VMEM((K3, n * X), BF16) for n in (9, 7, 7, 3, 5, 3)]
            + [
                pltpu.VMEM((3, YC, X), F32),
                pltpu.VMEM((YC, X), F32),
                pltpu.VMEM((5, YC, X), F32),
                pltpu.VMEM((6, YC, 3 * K3), BF16),
                pltpu.VMEM((6 * C, 14 * X), BF16),
                pltpu.SemaphoreType.DMA,
            ],
            vmem=52,
            flops=10**10,
            moved=10**7,
        ),
    )(arrived, blocks, bias)


def flip_swap(weight):
    return jnp.transpose(jnp.flip(weight, (2, 3, 4)), (1, 0, 2, 3, 4))


def for_each_sum(kernel, arrived, peers, dtype):
    return pl.pallas_call(
        kernel,
        in_specs=[vmem_spec()],
        out_specs=vmem_spec(),
        **call(kernel, jax.ShapeDtypeStruct((peers, 24, X), dtype), vmem=16),
    )(arrived)


def body(
    camera_feats,
    footprint_slot_weights,
    tile_bricks,
    tile_rows,
    conv_first,
    conv_second,
    conv_third,
    bias_first,
    bias_second,
    out_grad,
):
    depths, heights, views = (lax.axis_size(n) for n in ("depth", "height", "view"))
    tiles, slots = tile_bricks.shape

    partial = pl.pallas_call(
        lift_kernel,
        in_specs=[smem_spec(), smem_spec(), hbm_spec(), hbm_spec()],
        out_specs=vmem_spec(),
        **call(
            lift_kernel,
            jax.ShapeDtypeStruct((views, HALF, X), BF16),
            [
                pltpu.VMEM((tiles * C, X), BF16),
                pltpu.VMEM((slots, X, X), BF16),
                pltpu.VMEM((views * YB, C, X), F32),
                pltpu.SemaphoreType.DMA((2,)),
            ],
            vmem=62,
            flops=10**8,
            moved=10**6,
        ),
    )(tile_bricks, tile_rows, camera_feats.reshape(tiles * C, X), footprint_slot_weights)
    pieces = lax.all_to_all(partial, "view", 0, 0, tiled=True)

    convs = [conv_first, conv_second, conv_third]
    convs = jnp.stack(convs + [flip_swap(w) for w in reversed(convs)])
    taps = jnp.transpose(convs, (0, 1, 3, 5, 4, 2)).reshape(6 * C, 27 * C)
    taps = jnp.pad(taps, ((0, 0), (0, 4 * X - 27 * C)))
    blocks = pl.pallas_call(
        block_kernel,
        in_specs=[vmem_spec()] * 2,
        out_specs=vmem_spec(),
        **call(
            block_kernel,
            jax.ShapeDtypeStruct((6 * C, 14 * X), BF16),
            flops=10**8,
            moved=10**6,
        ),
    )(taps, block_places())
    bias = jnp.stack([jnp.tile(b, YC // C) for b in (bias_first, bias_second)])[:, :, None]

    own = pl.pallas_call(
        own_kernel,
        in_specs=[vmem_spec()] * 2,
        out_specs=vmem_spec(),
        **call(own_kernel, jax.ShapeDtypeStruct((2, HALF, X), BF16), vmem=16),
    )(pieces, out_grad.reshape(HALF, X))
    moves = []
    for d in range(depths):
        for v in range(views):
            to = d + (1 if v >= views // 2 else -1)
            if 0 <= to < depths:
                moves.append((d * views + v, to * views + v))
    far = lax.ppermute(own, ("depth", "view"), moves)
    facing = pl.pallas_call(
        facing_kernel,
        in_specs=[vmem_spec()] * 2,
        out_specs=vmem_spec(),
        **call(facing_kernel, jax.ShapeDtypeStruct((4, RIM, X), BF16)),
    )(own, far)
    rim = lax.ppermute(facing, "height", [(0, 1), (1, 0)])
    parts = pl.pallas_call(
        parts_kernel,
        in_specs=[vmem_spec()] * 3,
        out_specs=vmem_spec(),
        **call(
            parts_kernel,
            jax.ShapeDtypeStruct((VIEWS, 2, YC, X), BF16),
            [pltpu.VMEM((4, YC, X), BF16)],
        ),
    )(own, far, rim)
    arrived = lax.all_to_all(parts, "view", 0, 0, tiled=True)

    field, payload = main_call(arrived, blocks, bias)
    arrived = lax.all_to_all(payload, "view", 0, 0, tiled=True)

    across = ("depth", "height")
    sums = for_each_sum(first_sum_kernel, arrived, depths * heights, BF16)
    sums = lax.all_to_all(sums, across, 0, 0, tiled=True)
    sums = for_each_sum(next_sum_kernel, sums, views, F32)

    camera_grad = pl.pallas_call(
        camera_kernel,
        in_specs=[smem_spec(), smem_spec(), vmem_spec(), vmem_spec()],
        out_specs=vmem_spec(),
        **call(
            camera_kernel,
            jax.ShapeDtypeStruct((tiles * C, X), F32),
            [pltpu.VMEM((tiles * C, slots * X), BF16)],
            flops=10**8,
            moved=10**6,
        ),
    )(tile_bricks, tile_rows, arrived, footprint_slot_weights)

    sums = lax.all_to_all(sums, "view", 0, 0, tiled=True).reshape(12 * C, X)
    scale = 1.0 / math.sqrt(YB * X * depths * heights * views)
    weight_grads, bias_gradient_pair = pl.pallas_call(
        functools.partial(spread_kernel, scale),
        in_specs=[vmem_spec()],
        out_specs=[vmem_spec()] * 2,
        **call(
            spread_kernel,
            (jax.ShapeDtypeStruct((81, C, C), F32), jax.ShapeDtypeStruct((2, C), F32)),
        ),
    )(sums)
    weight_grads = jnp.transpose(weight_grads.reshape(3, 3, 3, 3, C, C), (0, 4, 5, 1, 2, 3))
    return (
        field.reshape(1, YB, C, X),
        camera_grad.reshape(tiles, C, X),
        weight_grads,
        bias_gradient_pair,
    )


def solution(mesh):
    in_specs = (
        P(("depth", "height", "view"), None, None),
        P(),
        P(("depth", "height", "view"), None),
        P(("depth", "height", "view"), None),
        P(),
        P(),
        P(),
        P(),
        P(),
        P(("depth", "view"), "height", None, None),
    )
    out_specs = (
        P(("depth", "view"), "height", None, None),
        P(("depth", "height", "view"), None, None),
        P(),
        P(),
    )
    return jax.shard_map(body, mesh=mesh, in_specs=in_specs, out_specs=out_specs, check_vma=False)
```

```python
import functools
import math

import jax
import jax.numpy as jnp
import numpy as np
from jax import lax
from jax.experimental import pallas as pl
from jax.experimental.pallas import tpu as pltpu
from jax.sharding import PartitionSpec as P

C = 16
X = 128
YB = 8
HALF = 128
RIM = 64
YC = HALF + RIM
K3 = 3 * YC
VIEWS = 8
F32, BF16 = jnp.float32, jnp.bfloat16
MIB = 1 << 20


def call(kernel, outs, scratch=(), vmem=32, flops=0, moved=0):
    return dict(
        out_shape=outs,
        scratch_shapes=list(scratch),
        compiler_params=pltpu.CompilerParams(vmem_limit_bytes=vmem * MIB),
        cost_estimate=pl.CostEstimate(flops=flops, bytes_accessed=moved, transcendentals=0),
    )


def vmem_spec():
    return pl.BlockSpec(memory_space=pltpu.VMEM)


def hbm_spec():
    return pl.BlockSpec(memory_space=pltpu.HBM)


def smem_spec():
    return pl.BlockSpec(memory_space=pltpu.SMEM)


def block_kernel(taps_ref, place_ref, block_ref):
    lane = lax.broadcasted_iota(jnp.int32, (4 * X, 14 * X), 1)
    spread = jnp.where(lane == place_ref[...], 1.0, 0.0).astype(BF16)
    block_ref[...] = jnp.dot(taps_ref[...], spread, preferred_element_type=F32).astype(BF16)


def block_places():
    a, c, b, i = np.indices((3, 3, 3, C)).reshape(4, -1)
    out = np.full((4 * X, 1), -1, np.int32)
    out[: a.size, 0] = a * K3 + c * YC + b * C + i
    return out


def own_kernel(pieces_ref, grad_ref, own_ref):
    own_ref[0] = pieces_ref[...].astype(F32).sum(axis=0).astype(BF16)
    own_ref[1] = grad_ref[...]


def facing_kernel(own_ref, far_ref, facing_ref):
    at = pl.multiple_of((1 - lax.axis_index("height")) * RIM, RIM)
    facing_ref[0:2] = own_ref[:, pl.ds(at, RIM), :]
    facing_ref[2:4] = far_ref[:, pl.ds(at, RIM), :]


def parts_kernel(own_ref, far_ref, rim_ref, parts_ref, planes):
    height, view = lax.axis_index("height"), lax.axis_index("view")
    own_at = pl.multiple_of(height * RIM, RIM)
    rim_at = pl.multiple_of((1 - height) * HALF, RIM)
    planes[0:2, pl.ds(own_at, HALF), :] = own_ref[...]
    planes[2:4, pl.ds(own_at, HALF), :] = far_ref[...]
    planes[:, pl.ds(rim_at, RIM), :] = rim_ref[...]
    half = VIEWS // 2
    for v in range(VIEWS):
        away = jnp.abs(v - view)
        parts_ref[v, 0] = planes[jnp.where(away <= half, 0, 2)]
        parts_ref[v, 1] = planes[jnp.where(away == half, 2, jnp.where(away < half, 1, 3))]


def lift_kernel(bricks_ref, rows_ref, feats_hbm, weights_hbm, out_ref, feats, weights, total, sems):
    fetch_feats = pltpu.make_async_copy(feats_hbm, feats, sems.at[0])
    fetch_weights = pltpu.make_async_copy(weights_hbm, weights, sems.at[1])
    fetch_feats.start()
    fetch_weights.start()
    total[...] = jnp.zeros_like(total)
    tiles, slots = bricks_ref.shape
    fetch_feats.wait()
    fetch_weights.wait()
    for k in range(slots):
        blocks = lax.dot_general(
            feats[...], weights[k], (((1,), (1,)), ((), ())), preferred_element_type=F32
        )
        for t in range(tiles):
            total[bricks_ref[t, k] * YB + rows_ref[t, k]] += blocks[t * C : (t + 1) * C, :]
    out_ref[...] = total[...].astype(BF16).reshape(out_ref.shape)


def camera_kernel(bricks_ref, rows_ref, arrived_ref, weights_ref, out_ref, chosen):
    tiles, slots = bricks_ref.shape
    for k in range(slots):
        for t in range(tiles):
            at = pl.multiple_of(rows_ref[t, k] * C, C)
            chosen[t * C : (t + 1) * C, k * X : (k + 1) * X] = arrived_ref[
                jnp.bitwise_xor(bricks_ref[t, k], lax.axis_index("view")), pl.ds(at, C), :
            ]
    out_ref[...] = jnp.dot(
        chosen[...], weights_ref[...].reshape(slots * X, X), preferred_element_type=F32
    )


def first_sum_kernel(arrived_ref, out_ref):
    sums = arrived_ref[...].astype(F32).sum(axis=0)
    sums = sums[:24] + sums[24:]
    lost = sums - sums.astype(BF16).astype(F32)
    group = lax.broadcasted_iota(jnp.int32, sums.shape, 1) >> 4
    spare = jnp.logical_and(group >= 5, lax.axis_index("view") >= VIEWS - 2)
    sums = jnp.where(spare, pltpu.roll(lost, 2 * C, 1), sums).astype(BF16)
    out_ref[...] = jnp.broadcast_to(sums[None], out_ref.shape)


def next_sum_kernel(arrived_ref, out_ref):
    sums = arrived_ref[...].astype(F32).sum(axis=0, keepdims=True)
    out_ref[...] = jnp.broadcast_to(sums, out_ref.shape)


def spread_kernel(scale, sums_ref, weight_ref, bias_ref):
    for q in range(27):
        layer, a, c = q // 9, q // 3 % 3, q % 3
        for b in range(3):
            row = (q // 8 * 3 + b) * C
            block = sums_ref[row : row + C, q % 8 * C : (q % 8 + 1) * C]
            weight_ref[((layer * 3 + a) * 3 + b) * 3 + c] = block * scale
    for layer in range(2):
        lanes, lost = (slice((n + layer) * C, (n + 1 + layer) * C) for n in (3, 5))
        row = sums_ref[9 * C : 9 * C + 1, :]
        bias_ref[layer : layer + 1, :] = (row[:, lanes] + row[:, lost]) * scale


def silu_and_slope(v):
    s = jax.nn.sigmoid(v)
    return v * s, s * (1.0 + v * (1.0 - s))


def main_kernel(
    arrived_ref,
    block_hbm,
    bias_ref,
    field_ref,
    lift_ref,
    sums_ref,
    s_lift,
    s_grad,
    s_act1,
    s_act2,
    s_back2,
    s_back1,
    slope1,
    slope2,
    up2,
    band_ref,
    block_ref,
    sem,
):
    fetch_blocks = pltpu.make_async_copy(block_hbm, block_ref, sem)
    fetch_blocks.start()
    depth, height, view = (lax.axis_index(n) for n in ("depth", "height", "view"))
    lane = lax.broadcasted_iota(jnp.int32, (YC, X), 1)
    first_lane, last_lane = lane == 0, lane == X - 1
    low = height == 0

    def put(dst, index, plane):
        cols = slice(index * X, (index + 1) * X)
        dst[0:YC, cols] = jnp.where(first_lane, 0.0, pltpu.roll(plane, 1, 1)).astype(BF16)
        dst[YC : 2 * YC, cols] = plane.astype(BF16)
        dst[2 * YC : K3, cols] = jnp.where(last_lane, 0.0, pltpu.roll(plane, X - 1, 1)).astype(
            BF16
        )

    def fetch(offset, kind):
        source = lax.rem(view + offset + VIEWS, VIEWS)
        if offset == -4:
            kind = jnp.where(view < VIEWS // 2, 1, 0)
        if offset == 4:
            kind = jnp.where(view < VIEWS // 2, 0, 1)
        return arrived_ref[source, kind].astype(F32)

    def inside(offset):
        z = depth * VIEWS + view + offset
        return jnp.logical_and(z >= 0, z < lax.axis_size("depth") * VIEWS)

    def masked(offset, plane):
        return jnp.where(inside(offset), plane, 0.0)

    def conv(n, src, start, count):
        taken = [src[:, (start + a) * X : (start + a + count) * X] for a in range(3)]
        out = jnp.dot(band_ref[n], jnp.concatenate(taken, axis=0), preferred_element_type=F32)
        return [out[:, i * X : (i + 1) * X] for i in range(count)]

    own_at = pl.multiple_of(height * RIM, RIM)

    def conv_own(n, src):
        taken = [src[:, a * X : (a + 1) * X] for a in range(3)]
        return jnp.dot(
            band_ref[n, pl.ds(own_at, HALF), :],
            jnp.concatenate(taken, axis=0),
            preferred_element_type=F32,
        )

    def pairs(count):
        return [(i, min(2, count - i)) for i in range(0, count, 2)]

    for i in range(9):
        put(s_lift, i, fetch(i - 4, 0))
    for i in range(7):
        put(s_grad, i, fetch(i - 3, 1))

    fetch_blocks.wait()
    at = lax.broadcasted_iota(jnp.int32, (C, 14 * X), 1)
    below, above = at < 0, at < 0
    for w in range(9):
        start = w * YC
        below = jnp.logical_or(below, jnp.logical_and(at >= start, at < start + C))
        above = jnp.logical_or(above, jnp.logical_and(at >= start + 2 * C, at < start + 3 * C))
    for n in (0, 3, 1, 4, 5, 2):
        block = block_ref[n * C : (n + 1) * C, :].astype(F32)
        for y in range(YC // C):
            rows = block
            if y == 0:
                rows = jnp.where(below, 0.0, block)
            if y == YC // C - 1:
                rows = jnp.where(above, 0.0, block)
            if y != 1:
                rows = pltpu.roll(rows, (y - 1) * C % (14 * X), 1)
            band_ref[n, y * C : (y + 1) * C, :] = rows[:, : 3 * K3].astype(BF16)

    bias1, bias2 = bias_ref[0], bias_ref[1]
    for i, n in pairs(7):
        for j, pre in enumerate(conv(0, s_lift, i, n)):
            act, slope = silu_and_slope(pre + bias1)
            put(s_act1, i + j, masked(i + j - 3, act))
            if abs(i + j - 3) <= 1:
                slope1[i + j - 2] = slope
    for i, n in pairs(5):
        for j, up in enumerate(conv(3, s_grad, i, n)):
            up2[i + j] = up
    for i, n in pairs(5):
        for j, pre in enumerate(conv(1, s_act1, i, n)):
            at = i + j
            act, slope = silu_and_slope(pre + bias2)
            back = up2[at] * slope
            put(s_back2, at, masked(at - 2, back))
            if at == 2:
                slope2[...] = back
            if abs(at - 2) <= 1:
                before = s_act1[YC : 2 * YC, (at + 1) * X : (at + 2) * X].astype(F32)
                put(s_act2, at - 1, masked(at - 2, act + before))
    for i, n in pairs(3):
        for j, up in enumerate(conv(4, s_back2, i, n)):
            at = i + j
            back = (up2[at + 1] + up) * slope1[at]
            if at == 1:
                slope1[at] = back
            put(s_back1, at, masked(at - 1, back))

    def own_rows(plane):
        return jnp.where(low, plane[:HALF], plane[RIM:])

    lift_grad = conv_own(5, s_back1).astype(BF16)
    lift_ref[0] = lift_grad
    field_ref[...] = conv_own(2, s_act2).astype(BF16)

    wide = (HALF, K3)
    row_y = (lax.broadcasted_iota(jnp.int32, wide, 0) >> 4) + height * (RIM // C)
    col = lax.broadcasted_iota(jnp.int32, wide, 1)
    col_y = (col - jnp.where(col >= 2 * YC, 2 * YC, jnp.where(col >= YC, YC, 0))) >> 4
    bands = [col_y == row_y + (b - 1) for b in range(3)]
    group = lax.broadcasted_iota(jnp.int32, (3 * C, X), 1) // C
    left = lax.broadcasted_iota(jnp.int32, (3 * C, X), 1) < X // 2
    packed = [jnp.zeros((3 * C, X), F32) for _ in range(4)]
    layers = ((s_back1, 1, s_lift, 4), (s_back2, 2, s_act1, 3), (s_grad, 3, s_act2, 1))
    for layer, (g_ref, g_at, v_ref, v_at) in enumerate(layers):
        g = g_ref[pl.ds(YC + own_at, HALF), g_at * X : (g_at + 1) * X]
        for a in range(3):
            at = v_at + a - 1
            products = lax.dot_general(
                g,
                v_ref[:, at * X : (at + 1) * X],
                (((1,), (1,)), ((), ())),
                preferred_element_type=F32,
            )
            by_row = [
                jnp.where(band, products, 0.0).reshape(YB, C, K3).sum(axis=0) for band in bands
            ]
            by_row = jnp.concatenate(by_row, axis=0)
            end = jnp.concatenate([by_row[:, 4 * X :], jnp.zeros((3 * C, X // 2), F32)], axis=1)
            shared = by_row[:, X : 2 * X]
            parts = (
                by_row[:, :X] + jnp.where(left, shared, 0.0),
                by_row[:, 2 * X : 3 * X] + jnp.where(left, 0.0, shared),
                by_row[:, 3 * X : 4 * X] + end,
            )
            for c, part in enumerate(parts):
                for step in (64, 32, 16):
                    part = part + pltpu.roll(part, step, 1)
                q = (layer * 3 + a) * 3 + c
                packed[q // 8] = jnp.where(group == q % 8, part, packed[q // 8])
    for layer, plane in enumerate((slope1[1], slope2[...])):
        sums = jnp.sum(own_rows(plane), axis=1, keepdims=True)
        sums = jnp.broadcast_to(sums, (HALF, X)).reshape(YB, C, X).sum(axis=0)
        out_at = lax.broadcasted_iota(jnp.int32, (C, X), 0)
        to = lax.rem(lax.broadcasted_iota(jnp.int32, (C, X), 1), C)
        sums = jnp.sum(jnp.where(out_at == to, sums, 0.0), axis=0, keepdims=True)
        packed[3] = jnp.where(group == 3 + layer, jnp.broadcast_to(sums, (3 * C, X)), packed[3])
    for v in range(VIEWS):
        start = (v % 2) * 24
        rows = packed[v // 2][start : start + 24]
        high = rows.astype(BF16).astype(F32)
        both = jnp.concatenate([high, rows - high], axis=0)
        sums_ref[v] = both.astype(BF16)


def main_call(arrived, blocks, bias):
    return pl.pallas_call(
        main_kernel,
        in_specs=[vmem_spec(), hbm_spec(), vmem_spec()],
        out_specs=[vmem_spec()] * 3,
        **call(
            main_kernel,
            (
                jax.ShapeDtypeStruct((HALF, X), BF16),
                jax.ShapeDtypeStruct((1, HALF, X), BF16),
                jax.ShapeDtypeStruct((VIEWS, 48, X), BF16),
            ),
            [pltpu.VMEM((K3, n * X), BF16) for n in (9, 7, 7, 3, 5, 3)]
            + [
                pltpu.VMEM((3, YC, X), F32),
                pltpu.VMEM((YC, X), F32),
                pltpu.VMEM((5, YC, X), F32),
                pltpu.VMEM((6, YC, 3 * K3), BF16),
                pltpu.VMEM((6 * C, 14 * X), BF16),
                pltpu.SemaphoreType.DMA,
            ],
            vmem=52,
            flops=10**10,
            moved=10**7,
        ),
    )(arrived, blocks, bias)


def flip_swap(weight):
    return jnp.transpose(jnp.flip(weight, (2, 3, 4)), (1, 0, 2, 3, 4))


def for_each_sum(kernel, arrived, peers, dtype):
    return pl.pallas_call(
        kernel,
        in_specs=[vmem_spec()],
        out_specs=vmem_spec(),
        **call(kernel, jax.ShapeDtypeStruct((peers, 24, X), dtype), vmem=16),
    )(arrived)


def body(
    camera_feats,
    footprint_slot_weights,
    tile_bricks,
    tile_rows,
    conv_first,
    conv_second,
    conv_third,
    bias_first,
    bias_second,
    out_grad,
):
    depths, heights, views = (lax.axis_size(n) for n in ("depth", "height", "view"))
    tiles, slots = tile_bricks.shape

    partial = pl.pallas_call(
        lift_kernel,
        in_specs=[smem_spec(), smem_spec(), hbm_spec(), hbm_spec()],
        out_specs=vmem_spec(),
        **call(
            lift_kernel,
            jax.ShapeDtypeStruct((views, HALF, X), BF16),
            [
                pltpu.VMEM((tiles * C, X), BF16),
                pltpu.VMEM((slots, X, X), BF16),
                pltpu.VMEM((views * YB, C, X), F32),
                pltpu.SemaphoreType.DMA((2,)),
            ],
            vmem=62,
            flops=10**8,
            moved=10**6,
        ),
    )(tile_bricks, tile_rows, camera_feats.reshape(tiles * C, X), footprint_slot_weights)
    pieces = lax.all_to_all(partial, "view", 0, 0, tiled=True)

    convs = [conv_first, conv_second, conv_third]
    convs = jnp.stack(convs + [flip_swap(w) for w in reversed(convs)])
    taps = jnp.transpose(convs, (0, 1, 3, 5, 4, 2)).reshape(6 * C, 27 * C)
    taps = jnp.pad(taps, ((0, 0), (0, 4 * X - 27 * C)))
    blocks = pl.pallas_call(
        block_kernel,
        in_specs=[vmem_spec()] * 2,
        out_specs=vmem_spec(),
        **call(
            block_kernel,
            jax.ShapeDtypeStruct((6 * C, 14 * X), BF16),
            flops=10**8,
            moved=10**6,
        ),
    )(taps, block_places())
    bias = jnp.stack([jnp.tile(b, YC // C) for b in (bias_first, bias_second)])[:, :, None]

    own = pl.pallas_call(
        own_kernel,
        in_specs=[vmem_spec()] * 2,
        out_specs=vmem_spec(),
        **call(own_kernel, jax.ShapeDtypeStruct((2, HALF, X), BF16), vmem=16),
    )(pieces, out_grad.reshape(HALF, X))
    moves = []
    for d in range(depths):
        for v in range(views):
            to = d + (1 if v >= views // 2 else -1)
            if 0 <= to < depths:
                moves.append((d * views + v, to * views + v))
    far = lax.ppermute(own, ("depth", "view"), moves)
    facing = pl.pallas_call(
        facing_kernel,
        in_specs=[vmem_spec()] * 2,
        out_specs=vmem_spec(),
        **call(facing_kernel, jax.ShapeDtypeStruct((4, RIM, X), BF16)),
    )(own, far)
    rim = lax.ppermute(facing, "height", [(0, 1), (1, 0)])
    parts = pl.pallas_call(
        parts_kernel,
        in_specs=[vmem_spec()] * 3,
        out_specs=vmem_spec(),
        **call(
            parts_kernel,
            jax.ShapeDtypeStruct((VIEWS, 2, YC, X), BF16),
            [pltpu.VMEM((4, YC, X), BF16)],
        ),
    )(own, far, rim)
    arrived = lax.all_to_all(parts, "view", 0, 0, tiled=True)

    field, lift_grad, sums = main_call(arrived, blocks, bias)
    sums = lax.all_to_all(sums, "view", 0, 0, tiled=True)

    across = ("depth", "height")
    sums = for_each_sum(first_sum_kernel, sums, depths * heights, BF16)
    sums, lift_grad = lax.optimization_barrier((sums, lift_grad))
    for step in (1, 2, 4):
        pairs = [(v, v ^ step) for v in range(views)]
        lift_grad = jnp.concatenate([lift_grad, lax.ppermute(lift_grad, "view", pairs)])
    sums = lax.all_to_all(sums, across, 0, 0, tiled=True)
    sums = for_each_sum(next_sum_kernel, sums, views, F32)

    camera_grad = pl.pallas_call(
        camera_kernel,
        in_specs=[smem_spec(), smem_spec(), vmem_spec(), vmem_spec()],
        out_specs=vmem_spec(),
        **call(
            camera_kernel,
            jax.ShapeDtypeStruct((tiles * C, X), F32),
            [pltpu.VMEM((tiles * C, slots * X), BF16)],
            flops=10**8,
            moved=10**6,
        ),
    )(tile_bricks, tile_rows, lift_grad, footprint_slot_weights)

    sums = lax.all_to_all(sums, "view", 0, 0, tiled=True).reshape(12 * C, X)
    scale = 1.0 / math.sqrt(YB * X * depths * heights * views)
    weight_grads, bias_gradient_pair = pl.pallas_call(
        functools.partial(spread_kernel, scale),
        in_specs=[vmem_spec()],
        out_specs=[vmem_spec()] * 2,
        **call(
            spread_kernel,
            (jax.ShapeDtypeStruct((81, C, C), F32), jax.ShapeDtypeStruct((2, C), F32)),
        ),
    )(sums)
    weight_grads = jnp.transpose(weight_grads.reshape(3, 3, 3, 3, C, C), (0, 4, 5, 1, 2, 3))
    return (
        field.reshape(1, YB, C, X),
        camera_grad.reshape(tiles, C, X),
        weight_grads,
        bias_gradient_pair,
    )


def solution(mesh):
    in_specs = (
        P(("depth", "height", "view"), None, None),
        P(),
        P(("depth", "height", "view"), None),
        P(("depth", "height", "view"), None),
        P(),
        P(),
        P(),
        P(),
        P(),
        P(("depth", "view"), "height", None, None),
    )
    out_specs = (
        P(("depth", "view"), "height", None, None),
        P(("depth", "height", "view"), None, None),
        P(),
        P(),
    )
    return jax.shard_map(body, mesh=mesh, in_specs=in_specs, out_specs=out_specs, check_vma=False)
```

```python
import functools
import math

import jax
import jax.numpy as jnp
import numpy as np
from jax import lax
from jax.experimental import pallas as pl
from jax.experimental.pallas import tpu as pltpu
from jax.sharding import PartitionSpec as P

C = 16
X = 128
YB = 8
HALF = 128
RIM = 64
YC = HALF + RIM
K3 = 3 * YC
VIEWS = 8
F32, BF16 = jnp.float32, jnp.bfloat16
MIB = 1 << 20


def call(kernel, outs, scratch=(), vmem=32, flops=0, moved=0):
    return dict(
        out_shape=outs,
        scratch_shapes=list(scratch),
        compiler_params=pltpu.CompilerParams(vmem_limit_bytes=vmem * MIB),
        cost_estimate=pl.CostEstimate(flops=flops, bytes_accessed=moved, transcendentals=0),
    )


def vmem_spec():
    return pl.BlockSpec(memory_space=pltpu.VMEM)


def hbm_spec():
    return pl.BlockSpec(memory_space=pltpu.HBM)


def smem_spec():
    return pl.BlockSpec(memory_space=pltpu.SMEM)


def block_kernel(taps_ref, place_ref, block_ref):
    lane = lax.broadcasted_iota(jnp.int32, (4 * X, 14 * X), 1)
    spread = jnp.where(lane == place_ref[...], 1.0, 0.0).astype(BF16)
    block_ref[...] = jnp.dot(taps_ref[...], spread, preferred_element_type=F32).astype(BF16)


def block_places():
    a, c, b, i = np.indices((3, 3, 3, C)).reshape(4, -1)
    out = np.full((4 * X, 1), -1, np.int32)
    out[: a.size, 0] = a * K3 + c * YC + b * C + i
    return out


def own_kernel(pieces_ref, grad_ref, own_ref):
    own_ref[0] = pieces_ref[...].astype(F32).sum(axis=0).astype(BF16)
    own_ref[1] = grad_ref[...]


def facing_kernel(own_ref, far_ref, facing_ref):
    at = pl.multiple_of((1 - lax.axis_index("height")) * RIM, RIM)
    facing_ref[0:2] = own_ref[:, pl.ds(at, RIM), :]
    facing_ref[2:4] = far_ref[:, pl.ds(at, RIM), :]


def parts_kernel(own_ref, far_ref, rim_ref, parts_ref, planes):
    height, view = lax.axis_index("height"), lax.axis_index("view")
    own_at = pl.multiple_of(height * RIM, RIM)
    rim_at = pl.multiple_of((1 - height) * HALF, RIM)
    planes[0:2, pl.ds(own_at, HALF), :] = own_ref[...]
    planes[2:4, pl.ds(own_at, HALF), :] = far_ref[...]
    planes[:, pl.ds(rim_at, RIM), :] = rim_ref[...]
    half = VIEWS // 2
    for v in range(VIEWS):
        away = jnp.abs(v - view)
        parts_ref[v, 0] = planes[jnp.where(away <= half, 0, 2)]
        parts_ref[v, 1] = planes[jnp.where(away == half, 2, jnp.where(away < half, 1, 3))]


def lift_kernel(
    bricks_hbm,
    rows_hbm,
    feats_hbm,
    weights_hbm,
    out_ref,
    bricks_ref,
    rows_ref,
    feats,
    weights,
    total,
    sems,
):
    pairs = (bricks_hbm, bricks_ref), (rows_hbm, rows_ref), (feats_hbm, feats), (weights_hbm, weights)
    fetches = [pltpu.make_async_copy(*pair, sems.at[n]) for n, pair in enumerate(pairs)]
    for fetch in fetches:
        fetch.start()
    total[...] = jnp.zeros_like(total)
    tiles, slots = bricks_ref.shape
    for fetch in fetches:
        fetch.wait()
    for k in range(slots):
        blocks = lax.dot_general(
            feats[...], weights[k], (((1,), (1,)), ((), ())), preferred_element_type=F32
        )
        for t in range(tiles):
            total[bricks_ref[t, k] * YB + rows_ref[t, k]] += blocks[t * C : (t + 1) * C, :]
    out_ref[...] = total[...].astype(BF16).reshape(out_ref.shape)


def camera_kernel(bricks_ref, rows_ref, arrived_ref, weights_ref, out_ref, chosen):
    tiles, slots = bricks_ref.shape
    for k in range(slots):
        for t in range(tiles):
            at = pl.multiple_of(rows_ref[t, k] * C, C)
            chosen[t * C : (t + 1) * C, k * X : (k + 1) * X] = arrived_ref[
                jnp.bitwise_xor(bricks_ref[t, k], lax.axis_index("view")), pl.ds(at, C), :
            ]
    out_ref[...] = jnp.dot(
        chosen[...], weights_ref[...].reshape(slots * X, X), preferred_element_type=F32
    )


def first_sum_kernel(arrived_ref, out_ref):
    sums = arrived_ref[...].astype(F32).sum(axis=0)
    sums = sums[:24] + sums[24:]
    lost = sums - sums.astype(BF16).astype(F32)
    group = lax.broadcasted_iota(jnp.int32, sums.shape, 1) >> 4
    spare = jnp.logical_and(group >= 5, lax.axis_index("view") >= VIEWS - 2)
    sums = jnp.where(spare, pltpu.roll(lost, 2 * C, 1), sums).astype(BF16)
    out_ref[...] = jnp.broadcast_to(sums[None], out_ref.shape)


def next_sum_kernel(arrived_ref, out_ref):
    sums = arrived_ref[...].astype(F32).sum(axis=0, keepdims=True)
    out_ref[...] = jnp.broadcast_to(sums, out_ref.shape)


def spread_kernel(scale, sums_ref, weight_ref, bias_ref):
    for q in range(27):
        layer, a, c = q // 9, q // 3 % 3, q % 3
        for b in range(3):
            row = (q // 8 * 3 + b) * C
            block = sums_ref[row : row + C, q % 8 * C : (q % 8 + 1) * C]
            weight_ref[((layer * 3 + a) * 3 + b) * 3 + c] = block * scale
    for layer in range(2):
        lanes, lost = (slice((n + layer) * C, (n + 1 + layer) * C) for n in (3, 5))
        row = sums_ref[9 * C : 9 * C + 1, :]
        bias_ref[layer : layer + 1, :] = (row[:, lanes] + row[:, lost]) * scale


def silu_and_slope(v):
    s = jax.nn.sigmoid(v)
    return v * s, s * (1.0 + v * (1.0 - s))


def main_kernel(
    arrived_ref,
    block_hbm,
    bias_ref,
    field_ref,
    lift_ref,
    sums_ref,
    s_lift,
    s_grad,
    s_act1,
    s_act2,
    s_back2,
    s_back1,
    slope1,
    slope2,
    up2,
    band_ref,
    block_ref,
    sem,
):
    fetch_blocks = pltpu.make_async_copy(block_hbm, block_ref, sem)
    fetch_blocks.start()
    depth, height, view = (lax.axis_index(n) for n in ("depth", "height", "view"))
    lane = lax.broadcasted_iota(jnp.int32, (YC, X), 1)
    first_lane, last_lane = lane == 0, lane == X - 1
    low = height == 0

    def put(dst, index, plane):
        cols = slice(index * X, (index + 1) * X)
        dst[0:YC, cols] = jnp.where(first_lane, 0.0, pltpu.roll(plane, 1, 1)).astype(BF16)
        dst[YC : 2 * YC, cols] = plane.astype(BF16)
        dst[2 * YC : K3, cols] = jnp.where(last_lane, 0.0, pltpu.roll(plane, X - 1, 1)).astype(
            BF16
        )

    def fetch(offset, kind):
        source = lax.rem(view + offset + VIEWS, VIEWS)
        if offset == -4:
            kind = jnp.where(view < VIEWS // 2, 1, 0)
        if offset == 4:
            kind = jnp.where(view < VIEWS // 2, 0, 1)
        return arrived_ref[source, kind].astype(F32)

    def inside(offset):
        z = depth * VIEWS + view + offset
        return jnp.logical_and(z >= 0, z < lax.axis_size("depth") * VIEWS)

    def masked(offset, plane):
        return jnp.where(inside(offset), plane, 0.0)

    def conv(n, src, start, count):
        taken = [src[:, (start + a) * X : (start + a + count) * X] for a in range(3)]
        out = jnp.dot(band_ref[n], jnp.concatenate(taken, axis=0), preferred_element_type=F32)
        return [out[:, i * X : (i + 1) * X] for i in range(count)]

    own_at = pl.multiple_of(height * RIM, RIM)

    def conv_own(n, src):
        taken = [src[:, a * X : (a + 1) * X] for a in range(3)]
        return jnp.dot(
            band_ref[n, pl.ds(own_at, HALF), :],
            jnp.concatenate(taken, axis=0),
            preferred_element_type=F32,
        )

    def pairs(count):
        return [(i, min(2, count - i)) for i in range(0, count, 2)]

    for i in range(9):
        put(s_lift, i, fetch(i - 4, 0))
    for i in range(7):
        put(s_grad, i, fetch(i - 3, 1))

    fetch_blocks.wait()
    at = lax.broadcasted_iota(jnp.int32, (C, 14 * X), 1)
    below, above = at < 0, at < 0
    for w in range(9):
        start = w * YC
        below = jnp.logical_or(below, jnp.logical_and(at >= start, at < start + C))
        above = jnp.logical_or(above, jnp.logical_and(at >= start + 2 * C, at < start + 3 * C))
    for n in (0, 3, 1, 4, 5, 2):
        block = block_ref[n * C : (n + 1) * C, :].astype(F32)
        for y in range(YC // C):
            rows = block
            if y == 0:
                rows = jnp.where(below, 0.0, block)
            if y == YC // C - 1:
                rows = jnp.where(above, 0.0, block)
            if y != 1:
                rows = pltpu.roll(rows, (y - 1) * C % (14 * X), 1)
            band_ref[n, y * C : (y + 1) * C, :] = rows[:, : 3 * K3].astype(BF16)

    bias1, bias2 = bias_ref[0], bias_ref[1]
    for i, n in pairs(7):
        for j, pre in enumerate(conv(0, s_lift, i, n)):
            act, slope = silu_and_slope(pre + bias1)
            put(s_act1, i + j, masked(i + j - 3, act))
            if abs(i + j - 3) <= 1:
                slope1[i + j - 2] = slope
    for i, n in pairs(5):
        for j, up in enumerate(conv(3, s_grad, i, n)):
            up2[i + j] = up
    for i, n in pairs(5):
        for j, pre in enumerate(conv(1, s_act1, i, n)):
            at = i + j
            act, slope = silu_and_slope(pre + bias2)
            back = up2[at] * slope
            put(s_back2, at, masked(at - 2, back))
            if at == 2:
                slope2[...] = back
            if abs(at - 2) <= 1:
                before = s_act1[YC : 2 * YC, (at + 1) * X : (at + 2) * X].astype(F32)
                put(s_act2, at - 1, masked(at - 2, act + before))
    for i, n in pairs(3):
        for j, up in enumerate(conv(4, s_back2, i, n)):
            at = i + j
            back = (up2[at + 1] + up) * slope1[at]
            if at == 1:
                slope1[at] = back
            put(s_back1, at, masked(at - 1, back))

    def own_rows(plane):
        return jnp.where(low, plane[:HALF], plane[RIM:])

    lift_grad = conv_own(5, s_back1).astype(BF16)
    lift_ref[0] = lift_grad
    field_ref[...] = conv_own(2, s_act2).astype(BF16)

    wide = (HALF, K3)
    row_y = (lax.broadcasted_iota(jnp.int32, wide, 0) >> 4) + height * (RIM // C)
    col = lax.broadcasted_iota(jnp.int32, wide, 1)
    col_y = (col - jnp.where(col >= 2 * YC, 2 * YC, jnp.where(col >= YC, YC, 0))) >> 4
    bands = [col_y == row_y + (b - 1) for b in range(3)]
    group = lax.broadcasted_iota(jnp.int32, (3 * C, X), 1) // C
    left = lax.broadcasted_iota(jnp.int32, (3 * C, X), 1) < X // 2
    packed = [jnp.zeros((3 * C, X), F32) for _ in range(4)]
    layers = ((s_back1, 1, s_lift, 4), (s_back2, 2, s_act1, 3), (s_grad, 3, s_act2, 1))
    for layer, (g_ref, g_at, v_ref, v_at) in enumerate(layers):
        g = g_ref[pl.ds(YC + own_at, HALF), g_at * X : (g_at + 1) * X]
        for a in range(3):
            at = v_at + a - 1
            products = lax.dot_general(
                g,
                v_ref[:, at * X : (at + 1) * X],
                (((1,), (1,)), ((), ())),
                preferred_element_type=F32,
            )
            by_row = [
                jnp.where(band, products, 0.0).reshape(YB, C, K3).sum(axis=0) for band in bands
            ]
            by_row = jnp.concatenate(by_row, axis=0)
            end = jnp.concatenate([by_row[:, 4 * X :], jnp.zeros((3 * C, X // 2), F32)], axis=1)
            shared = by_row[:, X : 2 * X]
            parts = (
                by_row[:, :X] + jnp.where(left, shared, 0.0),
                by_row[:, 2 * X : 3 * X] + jnp.where(left, 0.0, shared),
                by_row[:, 3 * X : 4 * X] + end,
            )
            for c, part in enumerate(parts):
                for step in (64, 32, 16):
                    part = part + pltpu.roll(part, step, 1)
                q = (layer * 3 + a) * 3 + c
                packed[q // 8] = jnp.where(group == q % 8, part, packed[q // 8])
    for layer, plane in enumerate((slope1[1], slope2[...])):
        sums = jnp.sum(own_rows(plane), axis=1, keepdims=True)
        sums = jnp.broadcast_to(sums, (HALF, X)).reshape(YB, C, X).sum(axis=0)
        out_at = lax.broadcasted_iota(jnp.int32, (C, X), 0)
        to = lax.rem(lax.broadcasted_iota(jnp.int32, (C, X), 1), C)
        sums = jnp.sum(jnp.where(out_at == to, sums, 0.0), axis=0, keepdims=True)
        packed[3] = jnp.where(group == 3 + layer, jnp.broadcast_to(sums, (3 * C, X)), packed[3])
    for v in range(VIEWS):
        start = (v % 2) * 24
        rows = packed[v // 2][start : start + 24]
        high = rows.astype(BF16).astype(F32)
        both = jnp.concatenate([high, rows - high], axis=0)
        sums_ref[v] = both.astype(BF16)


def main_call(arrived, blocks, bias):
    return pl.pallas_call(
        main_kernel,
        in_specs=[vmem_spec(), hbm_spec(), vmem_spec()],
        out_specs=[vmem_spec()] * 3,
        **call(
            main_kernel,
            (
                jax.ShapeDtypeStruct((HALF, X), BF16),
                jax.ShapeDtypeStruct((1, HALF, X), BF16),
                jax.ShapeDtypeStruct((VIEWS, 48, X), BF16),
            ),
            [pltpu.VMEM((K3, n * X), BF16) for n in (9, 7, 7, 3, 5, 3)]
            + [
                pltpu.VMEM((3, YC, X), F32),
                pltpu.VMEM((YC, X), F32),
                pltpu.VMEM((5, YC, X), F32),
                pltpu.VMEM((6, YC, 3 * K3), BF16),
                pltpu.VMEM((6 * C, 14 * X), BF16),
                pltpu.SemaphoreType.DMA,
            ],
            vmem=52,
            flops=10**10,
            moved=10**7,
        ),
    )(arrived, blocks, bias)


def flip_swap(weight):
    return jnp.transpose(jnp.flip(weight, (2, 3, 4)), (1, 0, 2, 3, 4))


def for_each_sum(kernel, arrived, peers, dtype):
    return pl.pallas_call(
        kernel,
        in_specs=[vmem_spec()],
        out_specs=vmem_spec(),
        **call(kernel, jax.ShapeDtypeStruct((peers, 24, X), dtype), vmem=16),
    )(arrived)


def body(
    camera_feats,
    footprint_slot_weights,
    tile_bricks,
    tile_rows,
    conv_first,
    conv_second,
    conv_third,
    bias_first,
    bias_second,
    out_grad,
):
    depths, heights, views = (lax.axis_size(n) for n in ("depth", "height", "view"))
    tiles, slots = tile_bricks.shape

    partial = pl.pallas_call(
        lift_kernel,
        in_specs=[hbm_spec()] * 4,
        out_specs=vmem_spec(),
        **call(
            lift_kernel,
            jax.ShapeDtypeStruct((views, HALF, X), BF16),
            [
                pltpu.SMEM((tiles, slots), jnp.int32),
                pltpu.SMEM((tiles, slots), jnp.int32),
                pltpu.VMEM((tiles * C, X), BF16),
                pltpu.VMEM((slots, X, X), BF16),
                pltpu.VMEM((views * YB, C, X), F32),
                pltpu.SemaphoreType.DMA((4,)),
            ],
            vmem=62,
            flops=10**8,
            moved=10**6,
        ),
    )(tile_bricks, tile_rows, camera_feats.reshape(tiles * C, X), footprint_slot_weights)
    pieces = lax.all_to_all(partial, "view", 0, 0, tiled=True)

    convs = [conv_first, conv_second, conv_third]
    convs = jnp.stack(convs + [flip_swap(w) for w in reversed(convs)])
    taps = jnp.transpose(convs, (0, 1, 3, 5, 4, 2)).reshape(6 * C, 27 * C)
    taps = jnp.pad(taps, ((0, 0), (0, 4 * X - 27 * C)))
    blocks = pl.pallas_call(
        block_kernel,
        in_specs=[vmem_spec()] * 2,
        out_specs=vmem_spec(),
        **call(
            block_kernel,
            jax.ShapeDtypeStruct((6 * C, 14 * X), BF16),
            flops=10**8,
            moved=10**6,
        ),
    )(taps, block_places())
    bias = jnp.stack([jnp.tile(b, YC // C) for b in (bias_first, bias_second)])[:, :, None]

    own = pl.pallas_call(
        own_kernel,
        in_specs=[vmem_spec()] * 2,
        out_specs=vmem_spec(),
        **call(own_kernel, jax.ShapeDtypeStruct((2, HALF, X), BF16), vmem=16),
    )(pieces, out_grad.reshape(HALF, X))
    moves = []
    for d in range(depths):
        for v in range(views):
            to = d + (1 if v >= views // 2 else -1)
            if 0 <= to < depths:
                moves.append((d * views + v, to * views + v))
    far = lax.ppermute(own, ("depth", "view"), moves)
    facing = pl.pallas_call(
        facing_kernel,
        in_specs=[vmem_spec()] * 2,
        out_specs=vmem_spec(),
        **call(facing_kernel, jax.ShapeDtypeStruct((4, RIM, X), BF16)),
    )(own, far)
    rim = lax.ppermute(facing, "height", [(0, 1), (1, 0)])
    parts = pl.pallas_call(
        parts_kernel,
        in_specs=[vmem_spec()] * 3,
        out_specs=vmem_spec(),
        **call(
            parts_kernel,
            jax.ShapeDtypeStruct((VIEWS, 2, YC, X), BF16),
            [pltpu.VMEM((4, YC, X), BF16)],
        ),
    )(own, far, rim)
    arrived = lax.all_to_all(parts, "view", 0, 0, tiled=True)

    field, lift_grad, sums = main_call(arrived, blocks, bias)
    sums = lax.all_to_all(sums, "view", 0, 0, tiled=True)

    across = ("depth", "height")
    sums = for_each_sum(first_sum_kernel, sums, depths * heights, BF16)
    sums, lift_grad = lax.optimization_barrier((sums, lift_grad))
    for step in (1, 2, 4):
        pairs = [(v, v ^ step) for v in range(views)]
        lift_grad = jnp.concatenate([lift_grad, lax.ppermute(lift_grad, "view", pairs)])
    sums = lax.all_to_all(sums, across, 0, 0, tiled=True)
    sums = for_each_sum(next_sum_kernel, sums, views, F32)

    camera_grad = pl.pallas_call(
        camera_kernel,
        in_specs=[smem_spec(), smem_spec(), vmem_spec(), vmem_spec()],
        out_specs=vmem_spec(),
        **call(
            camera_kernel,
            jax.ShapeDtypeStruct((tiles * C, X), F32),
            [pltpu.VMEM((tiles * C, slots * X), BF16)],
            flops=10**8,
            moved=10**6,
        ),
    )(tile_bricks, tile_rows, lift_grad, footprint_slot_weights)

    sums = lax.all_to_all(sums, "view", 0, 0, tiled=True).reshape(12 * C, X)
    scale = 1.0 / math.sqrt(YB * X * depths * heights * views)
    weight_grads, bias_gradient_pair = pl.pallas_call(
        functools.partial(spread_kernel, scale),
        in_specs=[vmem_spec()],
        out_specs=[vmem_spec()] * 2,
        **call(
            spread_kernel,
            (jax.ShapeDtypeStruct((81, C, C), F32), jax.ShapeDtypeStruct((2, C), F32)),
        ),
    )(sums)
    weight_grads = jnp.transpose(weight_grads.reshape(3, 3, 3, 3, C, C), (0, 4, 5, 1, 2, 3))
    return (
        field.reshape(1, YB, C, X),
        camera_grad.reshape(tiles, C, X),
        weight_grads,
        bias_gradient_pair,
    )


def solution(mesh):
    in_specs = (
        P(("depth", "height", "view"), None, None),
        P(),
        P(("depth", "height", "view"), None),
        P(("depth", "height", "view"), None),
        P(),
        P(),
        P(),
        P(),
        P(),
        P(("depth", "view"), "height", None, None),
    )
    out_specs = (
        P(("depth", "view"), "height", None, None),
        P(("depth", "height", "view"), None, None),
        P(),
        P(),
    )
    return jax.shard_map(body, mesh=mesh, in_specs=in_specs, out_specs=out_specs, check_vma=False)
```

```python
import functools
import math

import jax
import jax.numpy as jnp
import numpy as np
from jax import lax
from jax.experimental import pallas as pl
from jax.experimental.pallas import tpu as pltpu
from jax.sharding import PartitionSpec as P

C = 16
X = 128
YB = 8
HALF = 128
RIM = 64
YC = HALF + RIM
K3 = 3 * YC
VIEWS = 8
F32, BF16 = jnp.float32, jnp.bfloat16
MIB = 1 << 20


def call(kernel, outs, scratch=(), vmem=32, flops=0, moved=0):
    return dict(
        out_shape=outs,
        scratch_shapes=list(scratch),
        compiler_params=pltpu.CompilerParams(vmem_limit_bytes=vmem * MIB),
        cost_estimate=pl.CostEstimate(flops=flops, bytes_accessed=moved, transcendentals=0),
    )


def vmem_spec():
    return pl.BlockSpec(memory_space=pltpu.VMEM)


def hbm_spec():
    return pl.BlockSpec(memory_space=pltpu.HBM)


def smem_spec():
    return pl.BlockSpec(memory_space=pltpu.SMEM)


def block_kernel(taps_ref, place_ref, block_ref):
    lane = lax.broadcasted_iota(jnp.int32, (4 * X, 14 * X), 1)
    spread = jnp.where(lane == place_ref[...], 1.0, 0.0).astype(BF16)
    block_ref[...] = jnp.dot(taps_ref[...], spread, preferred_element_type=F32).astype(BF16)


def block_places():
    a, c, b, i = np.indices((3, 3, 3, C)).reshape(4, -1)
    out = np.full((4 * X, 1), -1, np.int32)
    out[: a.size, 0] = a * K3 + c * YC + b * C + i
    return out


def own_kernel(pieces_ref, grad_ref, own_ref):
    own_ref[0] = pieces_ref[...].astype(F32).sum(axis=0).astype(BF16)
    own_ref[1] = grad_ref[...]


def facing_kernel(own_ref, far_ref, facing_ref):
    at = pl.multiple_of((1 - lax.axis_index("height")) * RIM, RIM)
    facing_ref[0:2] = own_ref[:, pl.ds(at, RIM), :]
    facing_ref[2:4] = far_ref[:, pl.ds(at, RIM), :]


def parts_kernel(own_ref, far_ref, rim_ref, parts_ref, planes):
    height, view = lax.axis_index("height"), lax.axis_index("view")
    own_at = pl.multiple_of(height * RIM, RIM)
    rim_at = pl.multiple_of((1 - height) * HALF, RIM)
    planes[0:2, pl.ds(own_at, HALF), :] = own_ref[...]
    planes[2:4, pl.ds(own_at, HALF), :] = far_ref[...]
    planes[:, pl.ds(rim_at, RIM), :] = rim_ref[...]
    half = VIEWS // 2
    for v in range(VIEWS):
        away = jnp.abs(v - view)
        parts_ref[v, 0] = planes[jnp.where(away <= half, 0, 2)]
        parts_ref[v, 1] = planes[jnp.where(away == half, 2, jnp.where(away < half, 1, 3))]


def lift_kernel(
    bricks_hbm,
    rows_hbm,
    feats_hbm,
    weights_hbm,
    out_ref,
    bricks_ref,
    rows_ref,
    feats,
    weights,
    total,
    sems,
):
    pairs = (bricks_hbm, bricks_ref), (rows_hbm, rows_ref), (feats_hbm, feats), (weights_hbm, weights)
    fetches = [pltpu.make_async_copy(*pair, sems.at[n]) for n, pair in enumerate(pairs)]
    for fetch in fetches:
        fetch.start()
    total[...] = jnp.zeros_like(total)
    tiles, slots = bricks_ref.shape
    for fetch in fetches:
        fetch.wait()
    for k in range(slots):
        blocks = lax.dot_general(
            feats[...], weights[k], (((1,), (1,)), ((), ())), preferred_element_type=F32
        )
        for t in range(tiles):
            total[bricks_ref[t, k] * YB + rows_ref[t, k]] += blocks[t * C : (t + 1) * C, :]
    out_ref[...] = total[...].astype(BF16).reshape(out_ref.shape)


def reversed_bits(n):
    return ((n & 1) << 2) | (n & 2) | ((n >> 2) & 1)


def camera_kernel(bricks_ref, rows_ref, arrived_ref, weights_ref, out_ref, chosen):
    tiles, slots = bricks_ref.shape
    for k in range(slots):
        for t in range(tiles):
            at = pl.multiple_of(rows_ref[t, k] * C, C)
            chosen[t * C : (t + 1) * C, k * X : (k + 1) * X] = arrived_ref[
                reversed_bits(bricks_ref[t, k] ^ lax.axis_index("view")), pl.ds(at, C), :
            ]
    out_ref[...] = jnp.dot(
        chosen[...], weights_ref[...].reshape(slots * X, X), preferred_element_type=F32
    )


def first_sum_kernel(arrived_ref, out_ref):
    sums = arrived_ref[...].astype(F32).sum(axis=0)
    sums = sums[:24] + sums[24:]
    lost = sums - sums.astype(BF16).astype(F32)
    group = lax.broadcasted_iota(jnp.int32, sums.shape, 1) >> 4
    spare = jnp.logical_and(group >= 5, lax.axis_index("view") >= VIEWS - 2)
    sums = jnp.where(spare, pltpu.roll(lost, 2 * C, 1), sums).astype(BF16)
    out_ref[...] = jnp.broadcast_to(sums[None], out_ref.shape)


def next_sum_kernel(arrived_ref, out_ref):
    sums = arrived_ref[...].astype(F32).sum(axis=0, keepdims=True)
    out_ref[...] = jnp.broadcast_to(sums, out_ref.shape)


def spread_kernel(scale, sums_ref, weight_ref, bias_ref):
    for q in range(27):
        layer, a, c = q // 9, q // 3 % 3, q % 3
        for b in range(3):
            row = (q // 8 * 3 + b) * C
            block = sums_ref[row : row + C, q % 8 * C : (q % 8 + 1) * C]
            weight_ref[((layer * 3 + a) * 3 + b) * 3 + c] = block * scale
    for layer in range(2):
        lanes, lost = (slice((n + layer) * C, (n + 1 + layer) * C) for n in (3, 5))
        row = sums_ref[9 * C : 9 * C + 1, :]
        bias_ref[layer : layer + 1, :] = (row[:, lanes] + row[:, lost]) * scale


def silu_and_slope(v):
    s = jax.nn.sigmoid(v)
    return v * s, s * (1.0 + v * (1.0 - s))


def main_kernel(
    arrived_ref,
    block_hbm,
    bias_ref,
    field_ref,
    lift_ref,
    sums_ref,
    s_lift,
    s_grad,
    s_act1,
    s_act2,
    s_back2,
    s_back1,
    slope1,
    slope2,
    up2,
    band_ref,
    block_ref,
    sem,
):
    fetch_blocks = pltpu.make_async_copy(block_hbm, block_ref, sem)
    fetch_blocks.start()
    depth, height, view = (lax.axis_index(n) for n in ("depth", "height", "view"))
    lane = lax.broadcasted_iota(jnp.int32, (YC, X), 1)
    first_lane, last_lane = lane == 0, lane == X - 1
    low = height == 0

    def put(dst, index, plane):
        cols = slice(index * X, (index + 1) * X)
        dst[0:YC, cols] = jnp.where(first_lane, 0.0, pltpu.roll(plane, 1, 1)).astype(BF16)
        dst[YC : 2 * YC, cols] = plane.astype(BF16)
        dst[2 * YC : K3, cols] = jnp.where(last_lane, 0.0, pltpu.roll(plane, X - 1, 1)).astype(
            BF16
        )

    def fetch(offset, kind):
        source = lax.rem(view + offset + VIEWS, VIEWS)
        if offset == -4:
            kind = jnp.where(view < VIEWS // 2, 1, 0)
        if offset == 4:
            kind = jnp.where(view < VIEWS // 2, 0, 1)
        return arrived_ref[source, kind].astype(F32)

    def inside(offset):
        z = depth * VIEWS + view + offset
        return jnp.logical_and(z >= 0, z < lax.axis_size("depth") * VIEWS)

    def masked(offset, plane):
        return jnp.where(inside(offset), plane, 0.0)

    def conv(n, src, start, count):
        taken = [src[:, (start + a) * X : (start + a + count) * X] for a in range(3)]
        out = jnp.dot(band_ref[n], jnp.concatenate(taken, axis=0), preferred_element_type=F32)
        return [out[:, i * X : (i + 1) * X] for i in range(count)]

    own_at = pl.multiple_of(height * RIM, RIM)

    def conv_own(n, src):
        taken = [src[:, a * X : (a + 1) * X] for a in range(3)]
        return jnp.dot(
            band_ref[n, pl.ds(own_at, HALF), :],
            jnp.concatenate(taken, axis=0),
            preferred_element_type=F32,
        )

    def runs(count):
        return [(i, min(4, count - i)) for i in range(0, count, 4)]

    for i in range(9):
        put(s_lift, i, fetch(i - 4, 0))

    fetch_blocks.wait()
    at = lax.broadcasted_iota(jnp.int32, (C, 14 * X), 1)
    below, above = at < 0, at < 0
    for w in range(9):
        start = w * YC
        below = jnp.logical_or(below, jnp.logical_and(at >= start, at < start + C))
        above = jnp.logical_or(above, jnp.logical_and(at >= start + 2 * C, at < start + 3 * C))
    for n in (0, 3, 1, 4, 5, 2):
        block = block_ref[n * C : (n + 1) * C, :].astype(F32)
        for y in range(YC // C):
            rows = block
            if y == 0:
                rows = jnp.where(below, 0.0, block)
            if y == YC // C - 1:
                rows = jnp.where(above, 0.0, block)
            if y != 1:
                rows = pltpu.roll(rows, (y - 1) * C % (14 * X), 1)
            band_ref[n, y * C : (y + 1) * C, :] = rows[:, : 3 * K3].astype(BF16)

    bias1, bias2 = bias_ref[0], bias_ref[1]
    for i, n in runs(7):
        for j, pre in enumerate(conv(0, s_lift, i, n)):
            act, slope = silu_and_slope(pre + bias1)
            put(s_act1, i + j, masked(i + j - 3, act))
            if abs(i + j - 3) <= 1:
                slope1[i + j - 2] = slope
    for i in range(7):
        put(s_grad, i, fetch(i - 3, 1))
    for i, n in runs(5):
        for j, up in enumerate(conv(3, s_grad, i, n)):
            up2[i + j] = up
    for i, n in runs(5):
        for j, pre in enumerate(conv(1, s_act1, i, n)):
            at = i + j
            act, slope = silu_and_slope(pre + bias2)
            back = up2[at] * slope
            put(s_back2, at, masked(at - 2, back))
            if at == 2:
                slope2[...] = back
            if abs(at - 2) <= 1:
                before = s_act1[YC : 2 * YC, (at + 1) * X : (at + 2) * X].astype(F32)
                put(s_act2, at - 1, masked(at - 2, act + before))
    for i, n in runs(3):
        for j, up in enumerate(conv(4, s_back2, i, n)):
            at = i + j
            back = (up2[at + 1] + up) * slope1[at]
            if at == 1:
                slope1[at] = back
            put(s_back1, at, masked(at - 1, back))

    def own_rows(plane):
        return jnp.where(low, plane[:HALF], plane[RIM:])

    lift_grad = conv_own(5, s_back1).astype(BF16)
    lift_ref[0] = lift_grad
    field_ref[...] = conv_own(2, s_act2).astype(BF16)

    wide = (HALF, K3)
    row_y = (lax.broadcasted_iota(jnp.int32, wide, 0) >> 4) + height * (RIM // C)
    col = lax.broadcasted_iota(jnp.int32, wide, 1)
    col_y = (col - jnp.where(col >= 2 * YC, 2 * YC, jnp.where(col >= YC, YC, 0))) >> 4
    bands = [col_y == row_y + (b - 1) for b in range(3)]
    group = lax.broadcasted_iota(jnp.int32, (3 * C, X), 1) // C
    left = lax.broadcasted_iota(jnp.int32, (3 * C, X), 1) < X // 2
    packed = [jnp.zeros((3 * C, X), F32) for _ in range(4)]
    layers = ((s_back1, 1, s_lift, 4), (s_back2, 2, s_act1, 3), (s_grad, 3, s_act2, 1))
    for layer, (g_ref, g_at, v_ref, v_at) in enumerate(layers):
        g = g_ref[pl.ds(YC + own_at, HALF), g_at * X : (g_at + 1) * X]
        for a in range(3):
            at = v_at + a - 1
            products = lax.dot_general(
                g,
                v_ref[:, at * X : (at + 1) * X],
                (((1,), (1,)), ((), ())),
                preferred_element_type=F32,
            )
            by_row = [
                jnp.where(band, products, 0.0).reshape(YB, C, K3).sum(axis=0) for band in bands
            ]
            by_row = jnp.concatenate(by_row, axis=0)
            end = jnp.concatenate([by_row[:, 4 * X :], jnp.zeros((3 * C, X // 2), F32)], axis=1)
            shared = by_row[:, X : 2 * X]
            parts = (
                by_row[:, :X] + jnp.where(left, shared, 0.0),
                by_row[:, 2 * X : 3 * X] + jnp.where(left, 0.0, shared),
                by_row[:, 3 * X : 4 * X] + end,
            )
            for c, part in enumerate(parts):
                for step in (64, 32, 16):
                    part = part + pltpu.roll(part, step, 1)
                q = (layer * 3 + a) * 3 + c
                packed[q // 8] = jnp.where(group == q % 8, part, packed[q // 8])
    for layer, plane in enumerate((slope1[1], slope2[...])):
        sums = jnp.sum(own_rows(plane), axis=1, keepdims=True)
        sums = jnp.broadcast_to(sums, (HALF, X)).reshape(YB, C, X).sum(axis=0)
        out_at = lax.broadcasted_iota(jnp.int32, (C, X), 0)
        to = lax.rem(lax.broadcasted_iota(jnp.int32, (C, X), 1), C)
        sums = jnp.sum(jnp.where(out_at == to, sums, 0.0), axis=0, keepdims=True)
        packed[3] = jnp.where(group == 3 + layer, jnp.broadcast_to(sums, (3 * C, X)), packed[3])
    for v in range(VIEWS):
        start = (v % 2) * 24
        rows = packed[v // 2][start : start + 24]
        high = rows.astype(BF16).astype(F32)
        both = jnp.concatenate([high, rows - high], axis=0)
        sums_ref[v] = both.astype(BF16)


def main_call(arrived, blocks, bias):
    return pl.pallas_call(
        main_kernel,
        in_specs=[vmem_spec(), hbm_spec(), vmem_spec()],
        out_specs=[vmem_spec()] * 3,
        **call(
            main_kernel,
            (
                jax.ShapeDtypeStruct((HALF, X), BF16),
                jax.ShapeDtypeStruct((1, HALF, X), BF16),
                jax.ShapeDtypeStruct((VIEWS, 48, X), BF16),
            ),
            [pltpu.VMEM((K3, n * X), BF16) for n in (9, 7, 7, 3, 5, 3)]
            + [
                pltpu.VMEM((3, YC, X), F32),
                pltpu.VMEM((YC, X), F32),
                pltpu.VMEM((5, YC, X), F32),
                pltpu.VMEM((6, YC, 3 * K3), BF16),
                pltpu.VMEM((6 * C, 14 * X), BF16),
                pltpu.SemaphoreType.DMA,
            ],
            vmem=52,
            flops=10**10,
            moved=10**7,
        ),
    )(arrived, blocks, bias)


def flip_swap(weight):
    return jnp.transpose(jnp.flip(weight, (2, 3, 4)), (1, 0, 2, 3, 4))


def for_each_sum(kernel, arrived, peers, dtype):
    return pl.pallas_call(
        kernel,
        in_specs=[vmem_spec()],
        out_specs=vmem_spec(),
        **call(kernel, jax.ShapeDtypeStruct((peers, 24, X), dtype), vmem=16),
    )(arrived)


def body(
    camera_feats,
    footprint_slot_weights,
    tile_bricks,
    tile_rows,
    conv_first,
    conv_second,
    conv_third,
    bias_first,
    bias_second,
    out_grad,
):
    depths, heights, views = (lax.axis_size(n) for n in ("depth", "height", "view"))
    tiles, slots = tile_bricks.shape

    partial = pl.pallas_call(
        lift_kernel,
        in_specs=[hbm_spec()] * 4,
        out_specs=vmem_spec(),
        **call(
            lift_kernel,
            jax.ShapeDtypeStruct((views, HALF, X), BF16),
            [
                pltpu.SMEM((tiles, slots), jnp.int32),
                pltpu.SMEM((tiles, slots), jnp.int32),
                pltpu.VMEM((tiles * C, X), BF16),
                pltpu.VMEM((slots, X, X), BF16),
                pltpu.VMEM((views * YB, C, X), F32),
                pltpu.SemaphoreType.DMA((4,)),
            ],
            vmem=62,
            flops=10**8,
            moved=10**6,
        ),
    )(tile_bricks, tile_rows, camera_feats.reshape(tiles * C, X), footprint_slot_weights)
    pieces = lax.all_to_all(partial, "view", 0, 0, tiled=True)

    convs = [conv_first, conv_second, conv_third]
    convs = jnp.stack(convs + [flip_swap(w) for w in reversed(convs)])
    taps = jnp.transpose(convs, (0, 1, 3, 5, 4, 2)).reshape(6 * C, 27 * C)
    taps = jnp.pad(taps, ((0, 0), (0, 4 * X - 27 * C)))
    blocks = pl.pallas_call(
        block_kernel,
        in_specs=[vmem_spec()] * 2,
        out_specs=vmem_spec(),
        **call(
            block_kernel,
            jax.ShapeDtypeStruct((6 * C, 14 * X), BF16),
            flops=10**8,
            moved=10**6,
        ),
    )(taps, block_places())
    bias = jnp.stack([jnp.tile(b, YC // C) for b in (bias_first, bias_second)])[:, :, None]

    own = pl.pallas_call(
        own_kernel,
        in_specs=[vmem_spec()] * 2,
        out_specs=vmem_spec(),
        **call(own_kernel, jax.ShapeDtypeStruct((2, HALF, X), BF16), vmem=16),
    )(pieces, out_grad.reshape(HALF, X))
    moves = []
    for d in range(depths):
        for v in range(views):
            to = d + (1 if v >= views // 2 else -1)
            if 0 <= to < depths:
                moves.append((d * views + v, to * views + v))
    far = lax.ppermute(own, ("depth", "view"), moves)
    facing = pl.pallas_call(
        facing_kernel,
        in_specs=[vmem_spec()] * 2,
        out_specs=vmem_spec(),
        **call(facing_kernel, jax.ShapeDtypeStruct((4, RIM, X), BF16)),
    )(own, far)
    rim = lax.ppermute(facing, "height", [(0, 1), (1, 0)])
    parts = pl.pallas_call(
        parts_kernel,
        in_specs=[vmem_spec()] * 3,
        out_specs=vmem_spec(),
        **call(
            parts_kernel,
            jax.ShapeDtypeStruct((VIEWS, 2, YC, X), BF16),
            [pltpu.VMEM((4, YC, X), BF16)],
        ),
    )(own, far, rim)
    arrived = lax.all_to_all(parts, "view", 0, 0, tiled=True)

    field, lift_grad, sums = main_call(arrived, blocks, bias)
    sums = lax.all_to_all(sums, "view", 0, 0, tiled=True)

    across = ("depth", "height")
    sums = for_each_sum(first_sum_kernel, sums, depths * heights, BF16)
    sums, lift_grad = lax.optimization_barrier((sums, lift_grad))
    for step in (4, 2, 1):
        pairs = [(v, v ^ step) for v in range(views)]
        lift_grad = jnp.concatenate([lift_grad, lax.ppermute(lift_grad, "view", pairs)])
    sums = lax.all_to_all(sums, across, 0, 0, tiled=True)
    sums = for_each_sum(next_sum_kernel, sums, views, F32)

    camera_grad = pl.pallas_call(
        camera_kernel,
        in_specs=[smem_spec(), smem_spec(), vmem_spec(), vmem_spec()],
        out_specs=vmem_spec(),
        **call(
            camera_kernel,
            jax.ShapeDtypeStruct((tiles * C, X), F32),
            [pltpu.VMEM((tiles * C, slots * X), BF16)],
            flops=10**8,
            moved=10**6,
        ),
    )(tile_bricks, tile_rows, lift_grad, footprint_slot_weights)

    sums = lax.all_to_all(sums, "view", 0, 0, tiled=True).reshape(12 * C, X)
    scale = 1.0 / math.sqrt(YB * X * depths * heights * views)
    weight_grads, bias_gradient_pair = pl.pallas_call(
        functools.partial(spread_kernel, scale),
        in_specs=[vmem_spec()],
        out_specs=[vmem_spec()] * 2,
        **call(
            spread_kernel,
            (jax.ShapeDtypeStruct((81, C, C), F32), jax.ShapeDtypeStruct((2, C), F32)),
        ),
    )(sums)
    weight_grads = jnp.transpose(weight_grads.reshape(3, 3, 3, 3, C, C), (0, 4, 5, 1, 2, 3))
    return (
        field.reshape(1, YB, C, X),
        camera_grad.reshape(tiles, C, X),
        weight_grads,
        bias_gradient_pair,
    )


def solution(mesh):
    in_specs = (
        P(("depth", "height", "view"), None, None),
        P(),
        P(("depth", "height", "view"), None),
        P(("depth", "height", "view"), None),
        P(),
        P(),
        P(),
        P(),
        P(),
        P(("depth", "view"), "height", None, None),
    )
    out_specs = (
        P(("depth", "view"), "height", None, None),
        P(("depth", "height", "view"), None, None),
        P(),
        P(),
    )
    return jax.shard_map(body, mesh=mesh, in_specs=in_specs, out_specs=out_specs, check_vma=False)
```

```python
import functools
import math

import jax
import jax.numpy as jnp
import numpy as np
from jax import lax
from jax.experimental import pallas as pl
from jax.experimental.pallas import tpu as pltpu
from jax.sharding import PartitionSpec as P

C = 16
X = 128
YB = 8
HALF = 128
RIM = 64
YC = HALF + RIM
K3 = 3 * YC
VIEWS = 8
F32, BF16 = jnp.float32, jnp.bfloat16
MIB = 1 << 20


def call(kernel, outs, scratch=(), vmem=32, flops=0, moved=0):
    return dict(
        out_shape=outs,
        scratch_shapes=list(scratch),
        compiler_params=pltpu.CompilerParams(vmem_limit_bytes=vmem * MIB),
        cost_estimate=pl.CostEstimate(flops=flops, bytes_accessed=moved, transcendentals=0),
    )


def vmem_spec():
    return pl.BlockSpec(memory_space=pltpu.VMEM)


def hbm_spec():
    return pl.BlockSpec(memory_space=pltpu.HBM)


def smem_spec():
    return pl.BlockSpec(memory_space=pltpu.SMEM)


def block_kernel(taps_ref, place_ref, block_ref):
    lane = lax.broadcasted_iota(jnp.int32, (4 * X, 14 * X), 1)
    spread = jnp.where(lane == place_ref[...], 1.0, 0.0).astype(BF16)
    block_ref[...] = jnp.dot(taps_ref[...], spread, preferred_element_type=F32).astype(BF16)


def block_places():
    a, c, b, i = np.indices((3, 3, 3, C)).reshape(4, -1)
    out = np.full((4 * X, 1), -1, np.int32)
    out[: a.size, 0] = a * K3 + c * YC + b * C + i
    return out


def own_kernel(pieces_ref, grad_ref, own_ref):
    own_ref[0] = pieces_ref[...].astype(F32).sum(axis=0).astype(BF16)
    own_ref[1] = grad_ref[...]


def facing_kernel(own_ref, far_ref, facing_ref):
    at = pl.multiple_of((1 - lax.axis_index("height")) * RIM, RIM)
    facing_ref[0:2] = own_ref[:, pl.ds(at, RIM), :]
    facing_ref[2:4] = far_ref[:, pl.ds(at, RIM), :]


def parts_kernel(own_ref, far_ref, rim_ref, parts_ref, planes):
    height, view = lax.axis_index("height"), lax.axis_index("view")
    own_at = pl.multiple_of(height * RIM, RIM)
    rim_at = pl.multiple_of((1 - height) * HALF, RIM)
    planes[0:2, pl.ds(own_at, HALF), :] = own_ref[...]
    planes[2:4, pl.ds(own_at, HALF), :] = far_ref[...]
    planes[:, pl.ds(rim_at, RIM), :] = rim_ref[...]
    half = VIEWS // 2
    for v in range(VIEWS):
        away = jnp.abs(v - view)
        parts_ref[v, 0] = planes[jnp.where(away <= half, 0, 2)]
        parts_ref[v, 1] = planes[jnp.where(away == half, 2, jnp.where(away < half, 1, 3))]


def lift_kernel(
    bricks_hbm,
    rows_hbm,
    feats_hbm,
    weights_hbm,
    out_ref,
    bricks_ref,
    rows_ref,
    feats,
    weights,
    total,
    sems,
):
    pairs = (bricks_hbm, bricks_ref), (rows_hbm, rows_ref), (feats_hbm, feats), (weights_hbm, weights)
    fetches = [pltpu.make_async_copy(*pair, sems.at[n]) for n, pair in enumerate(pairs)]
    for fetch in fetches:
        fetch.start()
    total[...] = jnp.zeros_like(total)
    tiles, slots = bricks_ref.shape
    for fetch in fetches:
        fetch.wait()
    for k in range(slots):
        blocks = lax.dot_general(
            feats[...], weights[k], (((1,), (1,)), ((), ())), preferred_element_type=F32
        )
        for t in range(tiles):
            total[bricks_ref[t, k] * YB + rows_ref[t, k]] += blocks[t * C : (t + 1) * C, :]
    out_ref[...] = total[...].astype(BF16).reshape(out_ref.shape)


def camera_kernel(bricks_ref, rows_ref, arrived_ref, weights_ref, out_ref, chosen):
    tiles, slots = bricks_ref.shape
    for k in range(slots):
        for t in range(tiles):
            at = pl.multiple_of(rows_ref[t, k] * C, C)
            chosen[t * C : (t + 1) * C, k * X : (k + 1) * X] = arrived_ref[
                jnp.bitwise_xor(bricks_ref[t, k], lax.axis_index("view")), pl.ds(at, C), :
            ]
    out_ref[...] = jnp.dot(
        chosen[...], weights_ref[...].reshape(slots * X, X), preferred_element_type=F32
    )


def first_sum_kernel(arrived_ref, out_ref):
    sums = arrived_ref[...].astype(F32).sum(axis=0)
    sums = sums[:24] + sums[24:]
    lost = sums - sums.astype(BF16).astype(F32)
    group = lax.broadcasted_iota(jnp.int32, sums.shape, 1) >> 4
    spare = jnp.logical_and(group >= 5, lax.axis_index("view") >= VIEWS - 2)
    sums = jnp.where(spare, pltpu.roll(lost, 2 * C, 1), sums).astype(BF16)
    out_ref[...] = jnp.broadcast_to(sums[None], out_ref.shape)


def next_sum_kernel(arrived_ref, out_ref):
    sums = arrived_ref[...].astype(F32).sum(axis=0, keepdims=True)
    out_ref[...] = jnp.broadcast_to(sums, out_ref.shape)


def spread_kernel(scale, sums_ref, weight_ref, bias_ref):
    for q in range(27):
        layer, a, c = q // 9, q // 3 % 3, q % 3
        for b in range(3):
            row = (q // 8 * 3 + b) * C
            block = sums_ref[row : row + C, q % 8 * C : (q % 8 + 1) * C]
            weight_ref[((layer * 3 + a) * 3 + b) * 3 + c] = block * scale
    for layer in range(2):
        lanes, lost = (slice((n + layer) * C, (n + 1 + layer) * C) for n in (3, 5))
        row = sums_ref[9 * C : 9 * C + 1, :]
        bias_ref[layer : layer + 1, :] = (row[:, lanes] + row[:, lost]) * scale


def silu_and_slope(v):
    s = jax.nn.sigmoid(v)
    return v * s, s * (1.0 + v * (1.0 - s))


def main_kernel(
    arrived_ref,
    block_hbm,
    bias_ref,
    field_ref,
    lift_ref,
    sums_ref,
    s_lift,
    s_grad,
    s_act1,
    s_act2,
    s_back2,
    s_back1,
    slope1,
    slope2,
    up2,
    band_ref,
    block_ref,
    sem,
):
    fetch_blocks = pltpu.make_async_copy(block_hbm, block_ref, sem)
    fetch_blocks.start()
    depth, height, view = (lax.axis_index(n) for n in ("depth", "height", "view"))
    lane = lax.broadcasted_iota(jnp.int32, (YC, X), 1)
    first_lane, last_lane = lane == 0, lane == X - 1
    low = height == 0

    def put(dst, index, plane):
        cols = slice(index * X, (index + 1) * X)
        dst[0:YC, cols] = jnp.where(first_lane, 0.0, pltpu.roll(plane, 1, 1)).astype(BF16)
        dst[YC : 2 * YC, cols] = plane.astype(BF16)
        dst[2 * YC : K3, cols] = jnp.where(last_lane, 0.0, pltpu.roll(plane, X - 1, 1)).astype(
            BF16
        )

    def fetch(offset, kind):
        source = lax.rem(view + offset + VIEWS, VIEWS)
        if offset == -4:
            kind = jnp.where(view < VIEWS // 2, 1, 0)
        if offset == 4:
            kind = jnp.where(view < VIEWS // 2, 0, 1)
        return arrived_ref[source, kind].astype(F32)

    def inside(offset):
        z = depth * VIEWS + view + offset
        return jnp.logical_and(z >= 0, z < lax.axis_size("depth") * VIEWS)

    def masked(offset, plane):
        return jnp.where(inside(offset), plane, 0.0)

    def conv(n, src, start, count):
        taken = [src[:, (start + a) * X : (start + a + count) * X] for a in range(3)]
        out = jnp.dot(band_ref[n], jnp.concatenate(taken, axis=0), preferred_element_type=F32)
        return [out[:, i * X : (i + 1) * X] for i in range(count)]

    own_at = pl.multiple_of(height * RIM, RIM)

    def conv_own(n, src):
        taken = [src[:, a * X : (a + 1) * X] for a in range(3)]
        return jnp.dot(
            band_ref[n, pl.ds(own_at, HALF), :],
            jnp.concatenate(taken, axis=0),
            preferred_element_type=F32,
        )

    def pairs(count):
        return [(i, min(2, count - i)) for i in range(0, count, 2)]

    for i in range(9):
        put(s_lift, i, fetch(i - 4, 0))
    for i in range(7):
        put(s_grad, i, fetch(i - 3, 1))

    fetch_blocks.wait()
    at = lax.broadcasted_iota(jnp.int32, (C, 14 * X), 1)
    below, above = at < 0, at < 0
    for w in range(9):
        start = w * YC
        below = jnp.logical_or(below, jnp.logical_and(at >= start, at < start + C))
        above = jnp.logical_or(above, jnp.logical_and(at >= start + 2 * C, at < start + 3 * C))
    for n in (0, 3, 1, 4, 5, 2):
        block = block_ref[n * C : (n + 1) * C, :].astype(F32)
        for y in range(YC // C):
            rows = block
            if y == 0:
                rows = jnp.where(below, 0.0, block)
            if y == YC // C - 1:
                rows = jnp.where(above, 0.0, block)
            if y != 1:
                rows = pltpu.roll(rows, (y - 1) * C % (14 * X), 1)
            band_ref[n, y * C : (y + 1) * C, :] = rows[:, : 3 * K3].astype(BF16)

    bias1, bias2 = bias_ref[0], bias_ref[1]
    for i, n in pairs(7):
        for j, pre in enumerate(conv(0, s_lift, i, n)):
            act, slope = silu_and_slope(pre + bias1)
            put(s_act1, i + j, masked(i + j - 3, act))
            if abs(i + j - 3) <= 1:
                slope1[i + j - 2] = slope
    for i, n in pairs(5):
        for j, up in enumerate(conv(3, s_grad, i, n)):
            up2[i + j] = up
    for i, n in pairs(5):
        for j, pre in enumerate(conv(1, s_act1, i, n)):
            at = i + j
            act, slope = silu_and_slope(pre + bias2)
            back = up2[at] * slope
            put(s_back2, at, masked(at - 2, back))
            if at == 2:
                slope2[...] = back
            if abs(at - 2) <= 1:
                before = s_act1[YC : 2 * YC, (at + 1) * X : (at + 2) * X].astype(F32)
                put(s_act2, at - 1, masked(at - 2, act + before))
    for i, n in pairs(3):
        for j, up in enumerate(conv(4, s_back2, i, n)):
            at = i + j
            back = (up2[at + 1] + up) * slope1[at]
            if at == 1:
                slope1[at] = back
            put(s_back1, at, masked(at - 1, back))

    def own_rows(plane):
        return jnp.where(low, plane[:HALF], plane[RIM:])

    lift_grad = conv_own(5, s_back1).astype(BF16)
    lift_ref[0] = lift_grad
    field_ref[...] = conv_own(2, s_act2).astype(BF16)

    wide = (HALF, K3)
    row_y = (lax.broadcasted_iota(jnp.int32, wide, 0) >> 4) + height * (RIM // C)
    col = lax.broadcasted_iota(jnp.int32, wide, 1)
    col_y = (col - jnp.where(col >= 2 * YC, 2 * YC, jnp.where(col >= YC, YC, 0))) >> 4
    bands = [col_y == row_y + (b - 1) for b in range(3)]
    group = lax.broadcasted_iota(jnp.int32, (3 * C, X), 1) // C
    left = lax.broadcasted_iota(jnp.int32, (3 * C, X), 1) < X // 2
    packed = [jnp.zeros((3 * C, X), F32) for _ in range(4)]
    layers = ((s_back1, 1, s_lift, 4), (s_back2, 2, s_act1, 3), (s_grad, 3, s_act2, 1))
    for layer, (g_ref, g_at, v_ref, v_at) in enumerate(layers):
        g = g_ref[pl.ds(YC + own_at, HALF), g_at * X : (g_at + 1) * X]
        for a in range(3):
            at = v_at + a - 1
            products = lax.dot_general(
                g,
                v_ref[:, at * X : (at + 1) * X],
                (((1,), (1,)), ((), ())),
                preferred_element_type=F32,
            )
            by_row = [
                jnp.where(band, products, 0.0).reshape(YB, C, K3).sum(axis=0) for band in bands
            ]
            by_row = jnp.concatenate(by_row, axis=0)
            end = jnp.concatenate([by_row[:, 4 * X :], jnp.zeros((3 * C, X // 2), F32)], axis=1)
            shared = by_row[:, X : 2 * X]
            parts = (
                by_row[:, :X] + jnp.where(left, shared, 0.0),
                by_row[:, 2 * X : 3 * X] + jnp.where(left, 0.0, shared),
                by_row[:, 3 * X : 4 * X] + end,
            )
            for c, part in enumerate(parts):
                for step in (64, 32, 16):
                    part = part + pltpu.roll(part, step, 1)
                q = (layer * 3 + a) * 3 + c
                packed[q // 8] = jnp.where(group == q % 8, part, packed[q // 8])
    for layer, plane in enumerate((slope1[1], slope2[...])):
        sums = jnp.sum(own_rows(plane), axis=1, keepdims=True)
        sums = jnp.broadcast_to(sums, (HALF, X)).reshape(YB, C, X).sum(axis=0)
        out_at = lax.broadcasted_iota(jnp.int32, (C, X), 0)
        to = lax.rem(lax.broadcasted_iota(jnp.int32, (C, X), 1), C)
        sums = jnp.sum(jnp.where(out_at == to, sums, 0.0), axis=0, keepdims=True)
        packed[3] = jnp.where(group == 3 + layer, jnp.broadcast_to(sums, (3 * C, X)), packed[3])
    for v in range(VIEWS):
        start = (v % 2) * 24
        rows = packed[v // 2][start : start + 24]
        high = rows.astype(BF16).astype(F32)
        both = jnp.concatenate([high, rows - high], axis=0)
        sums_ref[v] = both.astype(BF16)


def main_call(arrived, blocks, bias):
    return pl.pallas_call(
        main_kernel,
        in_specs=[vmem_spec(), hbm_spec(), vmem_spec()],
        out_specs=[vmem_spec()] * 3,
        **call(
            main_kernel,
            (
                jax.ShapeDtypeStruct((HALF, X), BF16),
                jax.ShapeDtypeStruct((1, HALF, X), BF16),
                jax.ShapeDtypeStruct((VIEWS, 48, X), BF16),
            ),
            [pltpu.VMEM((K3, n * X), BF16) for n in (9, 7, 7, 3, 5, 3)]
            + [
                pltpu.VMEM((3, YC, X), F32),
                pltpu.VMEM((YC, X), F32),
                pltpu.VMEM((5, YC, X), F32),
                pltpu.VMEM((6, YC, 3 * K3), BF16),
                pltpu.VMEM((6 * C, 14 * X), BF16),
                pltpu.SemaphoreType.DMA,
            ],
            vmem=52,
            flops=10**10,
            moved=10**7,
        ),
    )(arrived, blocks, bias)


def flip_swap(weight):
    return jnp.transpose(jnp.flip(weight, (2, 3, 4)), (1, 0, 2, 3, 4))


def for_each_sum(kernel, arrived, peers, dtype):
    return pl.pallas_call(
        kernel,
        in_specs=[vmem_spec()],
        out_specs=vmem_spec(),
        **call(kernel, jax.ShapeDtypeStruct((peers, 24, X), dtype), vmem=16),
    )(arrived)


def body(
    camera_feats,
    footprint_slot_weights,
    tile_bricks,
    tile_rows,
    conv_first,
    conv_second,
    conv_third,
    bias_first,
    bias_second,
    out_grad,
):
    depths, heights, views = (lax.axis_size(n) for n in ("depth", "height", "view"))
    tiles, slots = tile_bricks.shape

    partial = pl.pallas_call(
        lift_kernel,
        in_specs=[hbm_spec()] * 4,
        out_specs=vmem_spec(),
        **call(
            lift_kernel,
            jax.ShapeDtypeStruct((views, HALF, X), BF16),
            [
                pltpu.SMEM((tiles, slots), jnp.int32),
                pltpu.SMEM((tiles, slots), jnp.int32),
                pltpu.VMEM((tiles * C, X), BF16),
                pltpu.VMEM((slots, X, X), BF16),
                pltpu.VMEM((views * YB, C, X), F32),
                pltpu.SemaphoreType.DMA((4,)),
            ],
            vmem=62,
            flops=10**8,
            moved=10**6,
        ),
    )(tile_bricks, tile_rows, camera_feats.reshape(tiles * C, X), footprint_slot_weights)
    pieces = lax.all_to_all(partial, "view", 0, 0, tiled=True)

    convs = [conv_first, conv_second, conv_third]
    convs = jnp.stack(convs + [flip_swap(w) for w in reversed(convs)])
    taps = jnp.transpose(convs, (0, 1, 3, 5, 4, 2)).reshape(6 * C, 27 * C)
    taps = jnp.pad(taps, ((0, 0), (0, 4 * X - 27 * C)))
    blocks = pl.pallas_call(
        block_kernel,
        in_specs=[vmem_spec()] * 2,
        out_specs=vmem_spec(),
        **call(
            block_kernel,
            jax.ShapeDtypeStruct((6 * C, 14 * X), BF16),
            flops=10**8,
            moved=10**6,
        ),
    )(taps, block_places())
    bias = jnp.stack([jnp.tile(b, YC // C) for b in (bias_first, bias_second)])[:, :, None]

    own = pl.pallas_call(
        own_kernel,
        in_specs=[vmem_spec()] * 2,
        out_specs=vmem_spec(),
        **call(own_kernel, jax.ShapeDtypeStruct((2, HALF, X), BF16), vmem=16),
    )(pieces, out_grad.reshape(HALF, X))
    moves = []
    for d in range(depths):
        for v in range(views):
            to = d + (1 if v >= views // 2 else -1)
            if 0 <= to < depths:
                moves.append((d * views + v, to * views + v))
    far = lax.ppermute(own, ("depth", "view"), moves)
    facing = pl.pallas_call(
        facing_kernel,
        in_specs=[vmem_spec()] * 2,
        out_specs=vmem_spec(),
        **call(facing_kernel, jax.ShapeDtypeStruct((4, RIM, X), BF16)),
    )(own, far)
    rim = lax.ppermute(facing, "height", [(0, 1), (1, 0)])
    parts = pl.pallas_call(
        parts_kernel,
        in_specs=[vmem_spec()] * 3,
        out_specs=vmem_spec(),
        **call(
            parts_kernel,
            jax.ShapeDtypeStruct((VIEWS, 2, YC, X), BF16),
            [pltpu.VMEM((4, YC, X), BF16)],
        ),
    )(own, far, rim)
    arrived = lax.all_to_all(parts, "view", 0, 0, tiled=True)

    field, lift_grad, sums = main_call(arrived, blocks, bias)
    sums = lax.all_to_all(sums, "view", 0, 0, tiled=True)

    across = ("depth", "height")
    sums = for_each_sum(first_sum_kernel, sums, depths * heights, BF16)
    pieces = lift_grad
    for step in (1, 2, 4):
        if step == 2:
            sums, pieces = lax.optimization_barrier((sums, pieces))
        pairs = [(v, v ^ step) for v in range(views)]
        pieces = jnp.concatenate([pieces, lax.ppermute(pieces, "view", pairs)])
    lift_grad = pieces
    sums = lax.all_to_all(sums, across, 0, 0, tiled=True)

    camera_grad = pl.pallas_call(
        camera_kernel,
        in_specs=[smem_spec(), smem_spec(), vmem_spec(), vmem_spec()],
        out_specs=vmem_spec(),
        **call(
            camera_kernel,
            jax.ShapeDtypeStruct((tiles * C, X), F32),
            [pltpu.VMEM((tiles * C, slots * X), BF16)],
            flops=10**8,
            moved=10**6,
        ),
    )(tile_bricks, tile_rows, lift_grad, footprint_slot_weights)

    sums, camera_grad = lax.optimization_barrier((sums, camera_grad))
    sums = for_each_sum(next_sum_kernel, sums, views, F32)
    sums = lax.all_to_all(sums, "view", 0, 0, tiled=True).reshape(12 * C, X)
    scale = 1.0 / math.sqrt(YB * X * depths * heights * views)
    weight_grads, bias_gradient_pair = pl.pallas_call(
        functools.partial(spread_kernel, scale),
        in_specs=[vmem_spec()],
        out_specs=[vmem_spec()] * 2,
        **call(
            spread_kernel,
            (jax.ShapeDtypeStruct((81, C, C), F32), jax.ShapeDtypeStruct((2, C), F32)),
        ),
    )(sums)
    weight_grads = jnp.transpose(weight_grads.reshape(3, 3, 3, 3, C, C), (0, 4, 5, 1, 2, 3))
    return (
        field.reshape(1, YB, C, X),
        camera_grad.reshape(tiles, C, X),
        weight_grads,
        bias_gradient_pair,
    )


def solution(mesh):
    in_specs = (
        P(("depth", "height", "view"), None, None),
        P(),
        P(("depth", "height", "view"), None),
        P(("depth", "height", "view"), None),
        P(),
        P(),
        P(),
        P(),
        P(),
        P(("depth", "view"), "height", None, None),
    )
    out_specs = (
        P(("depth", "view"), "height", None, None),
        P(("depth", "height", "view"), None, None),
        P(),
        P(),
    )
    return jax.shard_map(body, mesh=mesh, in_specs=in_specs, out_specs=out_specs, check_vma=False)
```
